128 devices in a mesh: exp: 8 (over x_lo, z), ten: 16 (over y, x_hi, core).
Axes of the slice: x: 4 (x_hi: 2, x_lo: 2; x = x_hi * 2 + x_lo), y: 4, z: 4, core: 2. Of those that a mesh axis runs over, the one named last changes fastest.
Arguments:
- master_gate_up: float32 [8, 2, 1536, 4096], P('exp', None, None, 'ten'), may hold values from -0.09375 to 0.09375
- grad_gate_up: float32 [8, 2, 1536, 4096], P('exp', None, None, 'ten'), may hold values from -24 to 24
- first_gate_up: float32 [8, 2, 1536, 4096], P('exp', None, None, 'ten'), may hold values from -3 to 3
- second_gate_up: float32 [8, 2, 1536, 4096], P('exp', None, None, 'ten'), may hold values from 1 to 16
- master_down: float32 [8, 1536, 4096], P('exp', None, 'ten'), may hold values from -0.15625 to 0.15625
- grad_down: float32 [8, 1536, 4096], P('exp', None, 'ten'), may hold values from -24 to 24
- first_down: float32 [8, 1536, 4096], P('exp', None, 'ten'), may hold values from -3 to 3
- second_down: float32 [8, 1536, 4096], P('exp', None, 'ten'), may hold values from 1 to 16
- tokens: bfloat16 [4096, 4096], P(('exp', 'ten')), may hold values from -6 to 6
- route_ids: int32 [4096, 2], P(('exp', 'ten')), may hold values from 0 to 7, all different within a row; in each aligned block of 32 rows (0 to 31, 32 to 63, ...) at most 12 rows name the same one
- route_weights: float32 [4096, 2], P(('exp', 'ten')), may hold values from 0.2 to 1
Outputs:
- new_master_gate_up: float32 [8, 2, 1536, 4096], P('exp', None, None, 'ten')
- new_master_down: float32 [8, 1536, 4096], P('exp', None, 'ten')
- rollout_gate_up: bfloat16 [8, 2, 1536, 4096], P('exp', None, 'ten')
- rollout_down: bfloat16 [8, 1536, 4096], P('exp', 'ten')
- moe_out: bfloat16 [4096, 4096], P(('exp', 'ten'))
The draws below stay inside these ranges and needn't reach their ends.
Inputs may be any that keep to these rules, and one draw needn't show every extreme that they name: `route_ids`: within one device's block of 32 rows no expert is named by more than 12 entries, a bound that some block reaches; a row names 2 different experts.
All inputs are finite; a program needn't handle non-finite values.
Results may differ from the reference program's by a relative error of at most 0.0033.
The reference program's roundings to bfloat16 on the way count: a program that leaves them out, or rounds other values in their place, can miss the bound.
Values may be sent and summed in bfloat16 or wider, within the bound.
No kernel may reach another device: no remote copies, remote signals or barrier semaphores. Data moves between devices by JAX's collectives and lax.ppermute only.
A program may use at most 192 MiB of HBM per device.

```python
import math
import jax
import jax.numpy as jnp
import numpy as np
from jax import lax

D = 4096
F = 1536
EXPERTS = 8
TOP = 2
ROWS_DEV = 32
CAP = 12
ROWS = 4096


def block_levels(stream_key, dims, shards, low, high):
    level = 1.0
    for axis_at, parts in shards:
        heights = jax.random.uniform(jax.random.fold_in(jax.random.fold_in(stream_key, 6), axis_at), (parts,), jnp.float32, low / len(shards), high / len(shards))
        level = level * jnp.repeat(jnp.exp(heights), dims[axis_at] // parts).reshape((-1,) + (1,) * (len(dims) - 1 - axis_at))
    return level


def shared_out(stream_key, own, number, rows, amount, top, most, slope):
    ranking = jax.random.permutation(stream_key, amount)
    packed, common = shares(amount, rows * top, most, slope, True), shares(amount, rows * top, most, slope, False)
    places = jnp.arange(amount)

    def named(lengths, turn):
        used = int((lengths > 0).sum())
        fixed = max(1, used // 4)
        passed = fixed + (places - fixed + turn * (used - fixed)) % max(1, amount - fixed)
        return jnp.zeros((amount,), jnp.int32).at[ranking[jnp.where(places < fixed, places, passed)]].set(jnp.asarray(lengths, jnp.int32))

    lengths = jnp.where(number % 4 == 0, named(packed, number // 4), named(common, number - number // 4 - 1))
    mixed = jax.random.permutation(jax.random.fold_in(own, 3), amount)
    donor, receiver = mixed[0:amount // 2 * 2:2], mixed[1:amount // 2 * 2:2]
    margin = jnp.minimum(lengths[donor] - 1, most - lengths[receiver]) // 2
    margin = jnp.where((donor == ranking[0]) | (receiver == ranking[0]) | (lengths[receiver] == 0), 0, jnp.maximum(margin, 0))
    passed = jax.random.randint(jax.random.fold_in(own, 4), (amount // 2,), 0, 1 << 20) % (margin + 1)
    lengths = lengths.at[donor].add(-passed).at[receiver].add(passed)
    members = jnp.searchsorted(jnp.cumsum(lengths), jnp.arange(rows * top), side="right").astype(jnp.int32)
    listing = members.reshape(top, rows).T
    listing = listing[jax.random.permutation(jax.random.fold_in(own, 1), rows)]
    turn = jax.random.randint(jax.random.fold_in(own, 2), (rows, 1), 0, top)
    return jnp.take_along_axis(listing, (jnp.arange(top)[None, :] + turn) % top, axis=1)


def shares(count, total, most, lean, full):
    loads = [(1 << 20) // math.isqrt(rank ** lean) + 1 for rank in range(1, count + 1)]
    largest = most if full else min(most, max(-(-total // count), total * loads[0] // sum(loads)))
    least = 1 if total - largest >= count - 1 else 0
    holding, spare = [largest] + [least] * (count - 1), total - largest - least * (count - 1)
    while spare > 0:
        movable = [i for i in range(1, count) if holding[i] < largest] or [i for i in range(1, count) if holding[i] < most]
        mass, left = sum([loads[i] for i in movable]), spare
        for i in movable:
            addition = min(most - holding[i], max(1, left * loads[i] // mass), spare)
            holding[i] = holding[i] + addition
            spare = spare - addition
    return np.array(holding)


def normal_values(key, extent, deviation, reach, cuts=(), kind=jnp.bfloat16):
    drawn = jax.random.normal(key, extent, jnp.float32) * deviation
    if len(cuts) > 0:
        drawn = block_levels(key, extent, cuts, -0.22, 0.18) * drawn
    return jnp.clip(drawn, min=-reach, max=reach).astype(kind)


def setup_inputs(seed: int = 0) -> dict:
    key_of = jax.random.split(jax.random.key(seed), 12)
    master_gate_up = normal_values(key_of[0], (EXPERTS, 2, F, D), D ** -0.5, 0.09375, ((0, 8), (3, 16)), jnp.float32)
    grad_gate_up = normal_values(key_of[1], (EXPERTS, 2, F, D), 4.0, 24.0, ((0, 8), (3, 16)), jnp.float32)
    first_gate_up = normal_values(key_of[2], (EXPERTS, 2, F, D), 0.5, 3.0, ((0, 8), (3, 16)), jnp.float32)
    second_gate_up = jnp.clip(jnp.exp(math.log(16.0) - 2.7725887 * jax.random.uniform(key_of[3], (EXPERTS, 2, F, D), jnp.float32) ** block_levels(key_of[3], (EXPERTS, 2, F, D), ((0, 8), (3, 16)), -0.2, 0.2)), 1.0, 16.0)
    master_down = normal_values(key_of[4], (EXPERTS, F, D), F ** -0.5, 0.15625, ((0, 8), (2, 16)), jnp.float32)
    grad_down = normal_values(key_of[5], (EXPERTS, F, D), 4.0, 24.0, ((0, 8), (2, 16)), jnp.float32)
    first_down = normal_values(key_of[6], (EXPERTS, F, D), 0.5, 3.0, ((0, 8), (2, 16)), jnp.float32)
    second_down = jnp.clip(jnp.exp(math.log(16.0) - 2.7725887 * jax.random.uniform(key_of[7], (EXPERTS, F, D), jnp.float32) ** block_levels(key_of[7], (EXPERTS, F, D), ((0, 8), (2, 16)), -0.2, 0.2)), 1.0, 16.0)
    tokens = normal_values(key_of[8], (ROWS, D), 1.0, 6.0, ((0, 128),))
    route_ids_keys = jax.random.split(jax.random.fold_in(key_of[9], 1), ROWS // ROWS_DEV)
    route_ids_turns = jax.random.permutation(jax.random.fold_in(key_of[9], 3), ROWS // ROWS_DEV)
    route_ids = jax.vmap(lambda own, number: shared_out(jax.random.fold_in(key_of[9], 2), own, number, ROWS_DEV, EXPERTS, TOP, CAP, 1))(route_ids_keys, route_ids_turns).reshape((ROWS, TOP))
    route_weights = jnp.clip(0.2 + 0.8 * jax.random.uniform(key_of[10], (ROWS, TOP), jnp.float32) ** block_levels(key_of[10], (ROWS, TOP), ((0, 128),), -0.2, 0.2), 0.2, 1.0)
    return {"master_gate_up": master_gate_up, "grad_gate_up": grad_gate_up, "first_gate_up": first_gate_up, "second_gate_up": second_gate_up, "master_down": master_down, "grad_down": grad_down, "first_down": first_down, "second_down": second_down, "tokens": tokens, "route_ids": route_ids, "route_weights": route_weights}


beta_first = 0.9
beta_second = 0.95
learn_rate = 0.01
weight_decay = 0.1
adam_epsilon = 1e-08
bias_first = 1.0 - 0.9 ** 50
bias_second = 1.0 - 0.95 ** 50

def adamw_update(master, grads, first, second):
    moment_one = beta_first * first + (1.0 - beta_first) * grads
    moment_two = beta_second * second + (1.0 - beta_second) * grads * grads
    scaled = moment_one / bias_first / (jnp.sqrt(moment_two / bias_second) + adam_epsilon)
    return master - learn_rate * (scaled + weight_decay * master)

def expert_apply(inputs):
    rows_in, gate_up, down = inputs
    flat = rows_in.reshape(-1, D)
    gate = jnp.dot(flat, gate_up[0].T, preferred_element_type=jnp.float32)
    up = jnp.dot(flat, gate_up[1].T, preferred_element_type=jnp.float32)
    hidden = (jax.nn.silu(gate) * up).astype(jnp.bfloat16)
    result = jnp.dot(hidden, down, preferred_element_type=jnp.float32).astype(jnp.bfloat16)
    return result.reshape(rows_in.shape)

def reference(master_gate_up, grad_gate_up, first_gate_up, second_gate_up, master_down, grad_down, first_down, second_down, tokens, route_ids, route_weights):
    new_master_gate_up = adamw_update(master_gate_up, grad_gate_up, first_gate_up, second_gate_up)
    new_master_down = adamw_update(master_down, grad_down, first_down, second_down)
    rollout_gate_up = new_master_gate_up.astype(jnp.bfloat16)
    rollout_down = new_master_down.astype(jnp.bfloat16)
    blocks = ROWS // ROWS_DEV
    grouped = route_ids.reshape(blocks, ROWS_DEV * TOP)
    onehot = (grouped[:, :, None] == jnp.arange(EXPERTS, dtype=jnp.int32)[None, None, :]).astype(jnp.int32)
    earlier = jnp.cumsum(onehot, axis=1) - onehot
    position = lax.optimization_barrier(jnp.sum(earlier * onehot, axis=2)).reshape(-1).astype(jnp.int32)
    flat_ids = route_ids.reshape(-1).astype(jnp.int32)
    entry_row = (jnp.arange(ROWS * TOP, dtype=jnp.int32) // TOP).astype(jnp.int32)
    entry_block = (entry_row // ROWS_DEV).astype(jnp.int32)
    buffer = jnp.zeros((EXPERTS, blocks, CAP, D), jnp.bfloat16)
    buffer = buffer.at[flat_ids, entry_block, position].set(tokens[entry_row])
    outputs = lax.map(expert_apply, (buffer, rollout_gate_up, rollout_down))
    picked = outputs[flat_ids, entry_block, position].reshape(ROWS, TOP, D).astype(jnp.float32)
    moe_out = lax.optimization_barrier(jnp.sum(route_weights[:, :, None] * picked, axis=1)).astype(jnp.bfloat16)
    return (new_master_gate_up, new_master_down, rollout_gate_up, rollout_down, moe_out)
```

```python
import functools

import jax
import jax.numpy as jnp
from jax import lax
from jax.experimental import pallas as pl
from jax.experimental.pallas import tpu as pltpu
from jax.sharding import PartitionSpec as P

beta_first = 0.9
beta_second = 0.95
learn_rate = 0.01
weight_decay = 0.1
adam_epsilon = 1e-08
bias_first = 1.0 - 0.9**50
bias_second = 1.0 - 0.95**50

F32 = jnp.float32
BF16 = jnp.bfloat16
VMEM = pl.BlockSpec(memory_space=pltpu.VMEM)
SMEM = pl.BlockSpec(memory_space=pltpu.SMEM)
ANY = pl.BlockSpec(memory_space=pl.ANY)
NT = (((1,), (1,)), ((), ()))

SHIFTS = (0, -1, 1, 2)
SLOTS = 12
PAIR = 2 * SLOTS


def adamw_update(master, grads, first, second):
    moment_one = beta_first * first + (1.0 - beta_first) * grads
    moment_two = beta_second * second + (1.0 - beta_second) * grads * grads
    scaled = moment_one * (1.0 / bias_first)
    scaled = scaled / (jnp.sqrt(moment_two * (1.0 / bias_second)) + adam_epsilon)
    return master - learn_rate * (scaled + weight_decay * master)


def params(mib=32):
    return pltpu.CompilerParams(vmem_limit_bytes=mib << 20)


def cost(flops, nbytes):
    return pl.CostEstimate(flops=int(flops), bytes_accessed=int(nbytes), transcendentals=0)


def move(array, target):
    pairs = []
    for i in range(128):
        xl, z, y, xh, core = i // 64, i // 16 % 4, i // 4 % 4, i // 2 % 2, i % 2
        a, b, c, d, f = target(xl, z, y, xh, core)
        pairs.append((i, ((a * 4 + b % 4) * 4 + c % 4) * 4 + d * 2 + f))
    return lax.ppermute(array, ("exp", "ten"), pairs)


def move_y(array, shift):
    return move(array, lambda xl, z, y, xh, core: (xl, z, y + shift, xh, core))


def move_xh(array):
    return move(array, lambda xl, z, y, xh, core: (xl, z, y, 1 - xh, core))


def move_core(array):
    return move(array, lambda xl, z, y, xh, core: (xl, z, y, xh, 1 - core))


def move_out(array, k):
    return move(array, lambda xl, z, y, xh, core: (core, z + k, y, xh, xl))


def move_home(array, k):
    return move(array, lambda xl, z, y, xh, core: (core, z - k, y, xh, xl))


def staged(arrays):
    return lax.optimization_barrier(arrays)


def after(arrays, others):
    return lax.optimization_barrier((arrays, others))[0]


def adam_kernel(count, parts, rows, blocks_ref, *refs):
    ins, rest = refs[:4], refs[4:]
    new_ref, pieces = rest[-(count + 5)], rest[-(count + 4) : -4]
    held_ref, made_ref, in_sem, out_sem = rest[-4:]
    steps = [(i, part) for i in range(count) for part in range(parts)]

    def at(ref, step):
        i, part = steps[step]
        return ref.at[0, part, pl.ds(pl.multiple_of(blocks_ref[i] * rows, rows), rows)]

    copies = [
        [
            pltpu.make_async_copy(at(ref, step), held_ref.at[step, j], in_sem.at[step, j])
            for j, ref in enumerate(ins)
        ]
        for step in range(len(steps))
    ]
    for step in copies:
        for copy in step:
            copy.start()
    outs = []
    for step, (i, part) in enumerate(steps):
        for copy in copies[step]:
            copy.wait()

        def some(r, carry, step=step, i=i, part=part):
            at_rows = pl.ds(pl.multiple_of(r * 32, 32), 32)
            new = adamw_update(*(held_ref[step, j, at_rows] for j in range(4)))
            made_ref[step, at_rows] = new
            pieces[i][part, at_rows] = new.astype(BF16)
            return carry

        lax.fori_loop(0, rows // 32, some, 0)
        out = pltpu.make_async_copy(made_ref.at[step], at(new_ref, step), out_sem.at[step])
        out.start()
        outs.append(out)
    for out in outs:
        out.wait()


def adam(blocks, arrays, target, rows):
    count, parts = blocks.shape[0], arrays[0].shape[1]
    given = [] if target is None else [target]
    return pl.pallas_call(
        functools.partial(adam_kernel, count, parts, rows),
        in_specs=[SMEM] + [ANY] * (4 + len(given)),
        out_specs=[ANY] + [VMEM] * count,
        out_shape=[jax.ShapeDtypeStruct(arrays[0].shape, F32)]
        + [jax.ShapeDtypeStruct((parts, rows, 256), BF16)] * count,
        scratch_shapes=[
            pltpu.VMEM((count * parts, 4, rows, 256), F32),
            pltpu.VMEM((count * parts, rows, 256), F32),
            pltpu.SemaphoreType.DMA((count * parts, 4)),
            pltpu.SemaphoreType.DMA((count * parts,)),
        ],
        input_output_aliases={5: 0} if given else {},
        cost_estimate=cost(0, count * parts * rows * 256 * 22),
        compiler_params=params(56),
        name="adam",
    )(blocks, *arrays, *given)


def slot_parts(slot):
    k = (slot >= PAIR).astype(jnp.int32) + (slot >= 2 * PAIR) + (slot >= 3 * PAIR)
    rest = slot - PAIR * k
    half = (rest >= SLOTS).astype(jnp.int32)
    return k, half, rest - SLOTS * half


def routing(where_ref, meta):
    rows = meta.shape[0]
    expert = lax.broadcasted_iota(jnp.int32, (rows, 128), 1).astype(F32)
    first = meta[:, 0:1] == expert
    second = meta[:, 1:2] == expert
    named = jnp.where(first | second, 1.0, 0.0)
    row = lax.broadcasted_iota(jnp.int32, (rows, rows), 0)
    column = lax.broadcasted_iota(jnp.int32, (rows, rows), 1)
    before = jnp.where(column < row, 1.0, 0.0)
    place = jnp.dot(before.astype(BF16), named.astype(BF16), preferred_element_type=F32)
    place = jnp.where(named > 0.0, place, 99.0)
    weight = jnp.where(first, meta[:, 2:3], 0.0) + jnp.where(second, meta[:, 3:4], 0.0)
    return place, weight


def expert_of_slot(where_ref):
    slot = lax.broadcasted_iota(jnp.int32, (96, 128), 0)
    expert = lax.broadcasted_iota(jnp.int32, (96, 128), 1)
    k, _, _ = slot_parts(slot)
    z = where_ref[4] + k
    z = jnp.where(z >= 4, z - 4, z)
    return jnp.where(expert == where_ref[2] * 4 + z, 1.0, 0.0).astype(BF16)


def dispatch_kernel(where_ref, own_ref, other_ref, own_meta_ref, other_meta_ref, *outs):
    at_expert = expert_of_slot(where_ref)
    slot = lax.broadcasted_iota(jnp.int32, (96, 32), 0)
    _, half, place_of_slot = slot_parts(slot)
    total = None
    for side, (rows_ref, meta_ref) in enumerate(
        ((own_ref, own_meta_ref), (other_ref, other_meta_ref))
    ):
        place, _ = routing(where_ref, meta_ref[...])
        found = lax.dot_general(at_expert, place.astype(BF16), NT, preferred_element_type=F32)
        hit = (found == place_of_slot.astype(F32)) & (half == side)
        placing = jnp.where(hit, 1.0, 0.0).astype(BF16)
        part = jnp.dot(placing, rows_ref[...], preferred_element_type=F32)
        total = part if total is None else total + part
    for k in range(4):
        outs[k][...] = total[k * PAIR : (k + 1) * PAIR].astype(BF16)


def dispatch(where, own, other, own_meta, other_meta):
    return pl.pallas_call(
        dispatch_kernel,
        in_specs=[SMEM] + [VMEM] * 4,
        out_specs=[VMEM] * 4,
        out_shape=[jax.ShapeDtypeStruct((PAIR, 4096), BF16)] * 4,
        cost_estimate=cost(2 * 96 * 64 * 4096, 4 << 20),
        compiler_params=params(),
        name="dispatch",
    )(where, own, other, own_meta, other_meta)


def combine_kernel(where_ref, own_meta_ref, other_meta_ref, *rest):
    backs, (own_ref, other_ref) = rest[:4], rest[4:]
    at_expert = expert_of_slot(where_ref)
    slot = lax.broadcasted_iota(jnp.int32, (32, 96), 1)
    _, half, place_of_slot = slot_parts(slot)
    parts = []
    for side, meta_ref in enumerate((own_meta_ref, other_meta_ref)):
        place, weight = routing(where_ref, meta_ref[...])
        found = lax.dot_general(place.astype(BF16), at_expert, NT, preferred_element_type=F32)
        hit = (found == place_of_slot.astype(F32)) & (half == side)
        left = weight
        for _ in range(3):
            piece = left.astype(BF16)
            left = left - piece.astype(F32)
            spread = lax.dot_general(piece, at_expert, NT, preferred_element_type=F32)
            parts.append(jnp.where(hit, spread, 0.0))
    mixing = jnp.concatenate(parts, axis=0).astype(BF16)
    for g, shift in enumerate(SHIFTS):
        lanes = pl.ds(g * 1024, 1024)
        back = jnp.concatenate([b[:, lanes].astype(F32) for b in backs], axis=0).astype(BF16)
        mixed = jnp.dot(mixing, back, preferred_element_type=F32)
        columns = pl.ds(pl.multiple_of(wrap(where_ref[0] - shift) * 1024, 1024), 1024)
        own_ref[:, columns] = mixed[0:32] + mixed[32:64] + mixed[64:96]
        other_ref[:, columns] = mixed[96:128] + mixed[128:160] + mixed[160:192]


def combine(where, own_meta, other_meta, backs):
    return pl.pallas_call(
        combine_kernel,
        in_specs=[SMEM] + [VMEM] * 6,
        out_specs=[VMEM] * 2,
        out_shape=[jax.ShapeDtypeStruct((32, 4096), F32)] * 2,
        cost_estimate=cost(2 * 192 * 96 * 4096, 2 << 20),
        compiler_params=params(),
        name="combine",
    )(where, own_meta, other_meta, *backs)


def wrap(y):
    y = jnp.where(y >= 4, y - 4, y)
    return jnp.where(y < 0, y + 4, y)


def first_kernel(where_ref, *refs):
    rows, pieces = refs[:8], refs[8:24]
    hidden_ref, rollout_ref, x_ref, w_ref, acc_ref, x_sem, w_sem, out_sem = refs[24:]
    y, xh, core = where_ref[0], where_ref[1], where_ref[2]
    x_copies = [
        pltpu.make_async_copy(rows[i], x_ref.at[pl.ds(i * 48, 48)], x_sem.at[i]) for i in range(8)
    ]
    w_copies = []
    for i in range(16):
        group, s = i // 4, i % 4
        from_y = wrap(y + SHIFTS[s])
        from_xh = xh if group % 2 == 0 else 1 - xh
        from_core = core if group < 2 else 1 - core
        columns = pl.ds(pl.multiple_of((from_y * 4 + from_xh * 2 + from_core) * 256, 256), 256)
        w_copies.append(pltpu.make_async_copy(pieces[i], w_ref.at[:, :, columns], w_sem.at[i]))
    for copy in x_copies:
        copy.start()
    for s in range(4):
        for group in range(4):
            w_copies[group * 4 + s].start()
    for copy in x_copies:
        copy.wait()
    for s in range(4):
        for group in range(4):
            w_copies[group * 4 + s].wait()
        columns = pl.ds(pl.multiple_of(wrap(y + SHIFTS[s]) * 1024, 1024), 1024)
        for g in range(2):
            product = lax.dot_general(
                x_ref[:, columns], w_ref[g, :, columns], NT, preferred_element_type=F32
            )
            if s == 0:
                acc_ref[g] = product
            else:
                acc_ref[g] += product
    out = pltpu.make_async_copy(
        w_ref.at[:, pl.ds(pl.multiple_of((xh * 2 + core) * 96, 96), 96), :],
        rollout_ref.at[0],
        out_sem,
    )
    out.start()
    gate, up = acc_ref[0], acc_ref[1]
    hidden_ref[...] = (gate / (1.0 + jnp.exp(-gate)) * up).astype(BF16)
    out.wait()


def first_matmul(where, rows, pieces):
    return pl.pallas_call(
        first_kernel,
        in_specs=[SMEM] + [ANY] * 24,
        out_specs=[VMEM, ANY],
        out_shape=[
            jax.ShapeDtypeStruct((384, 384), BF16),
            jax.ShapeDtypeStruct((1, 2, 96, 4096), BF16),
        ],
        scratch_shapes=[
            pltpu.VMEM((384, 4096), BF16),
            pltpu.VMEM((2, 384, 4096), BF16),
            pltpu.VMEM((2, 384, 384), F32),
            pltpu.SemaphoreType.DMA((8,)),
            pltpu.SemaphoreType.DMA((16,)),
            pltpu.SemaphoreType.DMA,
        ],
        cost_estimate=cost(2 * 384 * 768 * 4096, 11 << 20),
        compiler_params=params(),
        name="first_matmul",
    )(where, *rows, *pieces)


def second_kernel(where_ref, *refs):
    hidden, downs = refs[:4], refs[4:8]
    outs, slices = refs[8:12], refs[12:16]
    h_ref, d_ref, h_sem, d_sem, out_sem = refs[16:]
    y, xh, core = where_ref[0], where_ref[1], where_ref[2]
    copies = []
    for i in range(4):
        from_xh = xh if i % 2 == 0 else 1 - xh
        from_core = core if i < 2 else 1 - core
        columns = pl.ds(pl.multiple_of((from_xh * 2 + from_core) * 256, 256), 256)
        copies.append(pltpu.make_async_copy(downs[i], d_ref.at[:, columns], d_sem.at[i]))
    h_copies = []
    for d, shift in enumerate(SHIFTS):
        columns = pl.ds(pl.multiple_of(wrap(y + shift) * 384, 128), 384)
        for g, origin in enumerate(SHIFTS):
            there = [(s - origin + shift) % 4 for s in SHIFTS].index(0)
            h_copies.append(
                pltpu.make_async_copy(
                    hidden[d].at[pl.ds(there * 96, 96)],
                    h_ref.at[pl.ds(g * 96, 96), columns],
                    h_sem.at[d * 4 + g],
                )
            )
    for copy in copies + h_copies:
        copy.start()
    for copy in copies:
        copy.wait()
    sends = []
    for j, shift in enumerate(SHIFTS):
        first = pl.multiple_of((wrap(y + shift) * 4 + xh * 2 + core) * 96, 96)
        send = pltpu.make_async_copy(d_ref.at[pl.ds(first, 96)], slices[j], out_sem.at[j])
        send.start()
        sends.append(send)
    for copy in h_copies:
        copy.wait()
    for half in range(2):
        lanes = pl.ds(half * 512, 512)
        product = jnp.dot(h_ref[...], d_ref[:, lanes], preferred_element_type=F32).astype(BF16)
        for g in range(4):
            outs[g][:, lanes] = product[g * 96 : (g + 1) * 96]
    for send in sends:
        send.wait()


def second_matmul(where, hidden, downs):
    return pl.pallas_call(
        second_kernel,
        in_specs=[SMEM] + [ANY] * 8,
        out_specs=[VMEM] * 4 + [ANY] * 4,
        out_shape=[jax.ShapeDtypeStruct((96, 1024), BF16)] * 8,
        scratch_shapes=[
            pltpu.VMEM((384, 1536), BF16),
            pltpu.VMEM((1536, 1024), BF16),
            pltpu.SemaphoreType.DMA((16,)),
            pltpu.SemaphoreType.DMA((4,)),
            pltpu.SemaphoreType.DMA((4,)),
        ],
        cost_estimate=cost(2 * 384 * 1536 * 1024, 6 << 20),
        compiler_params=params(),
        name="second_matmul",
    )(where, *hidden, *downs)


def regroup_kernel(*refs):
    parts, outs = refs[:4], refs[4:]
    for g in range(4):
        wide = parts[g][...].astype(F32)
        for k in range(4):
            outs[k][:, g * 1024 : (g + 1) * 1024] = wide[k * PAIR : (k + 1) * PAIR].astype(BF16)


def regroup(parts):
    return pl.pallas_call(
        regroup_kernel,
        in_specs=[VMEM] * 4,
        out_specs=[VMEM] * 4,
        out_shape=[jax.ShapeDtypeStruct((PAIR, 4096), BF16)] * 4,
        cost_estimate=cost(0, 2 << 20),
        compiler_params=params(),
        name="regroup",
    )(*parts)


def place_kernel(where_ref, *refs):
    parts, out_ref, sem = refs[:4], refs[4], refs[5]
    copies = []
    for j, shift in enumerate(SHIFTS):
        columns = pl.ds(pl.multiple_of(wrap(where_ref[0] - shift) * 1024, 1024), 1024)
        copies.append(pltpu.make_async_copy(parts[j], out_ref.at[0, :, columns], sem.at[j]))
    for copy in copies:
        copy.start()
    for copy in copies:
        copy.wait()


def place_down(where, parts):
    return pl.pallas_call(
        place_kernel,
        in_specs=[SMEM] + [ANY] * 4,
        out_specs=ANY,
        out_shape=jax.ShapeDtypeStruct((1, 96, 4096), BF16),
        scratch_shapes=[pltpu.SemaphoreType.DMA((4,))],
        cost_estimate=cost(0, 2 << 20),
        compiler_params=params(),
        name="place_down",
    )(where, *parts)


def body(
    master_gate_up,
    grad_gate_up,
    first_gate_up,
    second_gate_up,
    master_down,
    grad_down,
    first_down,
    second_down,
    tokens,
    route_ids,
    route_weights,
):
    exp, ten = lax.axis_index("exp"), lax.axis_index("ten")
    y, xh, core, z = ten // 4, ten // 2 % 2, ten % 2, exp % 4
    where = jnp.stack([y, xh, core, exp // 4, z]).astype(jnp.int32)

    meta = jnp.concatenate([route_ids.astype(F32), route_weights], axis=1)
    other_tokens, other_meta = move_core(tokens), move_core(meta)

    gate_up = (master_gate_up, grad_gate_up, first_gate_up, second_gate_up)
    near = jnp.stack([(y + 1) % 4, (y + 3) % 4]).astype(jnp.int32)
    far = jnp.stack([y, (y + 2) % 4]).astype(jnp.int32)
    partial, to_next, to_last = adam(near, gate_up, None, 384)
    from_last, from_next = move_y(to_next, 1), move_y(to_last, -1)
    chunks = dispatch(where, tokens, other_tokens, meta, other_meta)
    arrived = [move_out(chunk, k) for k, chunk in enumerate(chunks)]
    partial = after(partial, chunks)
    new_master_gate_up, stays, to_far = adam(far, gate_up, partial, 384)
    down_arrays = tuple(a[:, None] for a in (master_down, grad_down, first_down, second_down))
    down_arrays = after(down_arrays, stays)
    new_master_down, down = adam(jnp.zeros((1,), jnp.int32), down_arrays, None, 1536)
    new_master_down, down = new_master_down[:, 0], down[0]

    stays_across = move_xh(stays)
    stays, from_last, from_next, stays_across, to_far, down = staged(
        (stays, from_last, from_next, stays_across, to_far, down)
    )
    from_far, last_across = move_y(to_far, 2), move_xh(from_last)
    crossed = {0: move_core(stays)}
    from_far, last_across, from_next, arrived, crossed[0], stays_across, from_last = staged(
        (from_far, last_across, from_next, arrived, crossed[0], stays_across, from_last)
    )
    head, tail = jnp.concatenate(arrived[:2], axis=0), jnp.concatenate(arrived[2:], axis=0)
    last_head, next_tail, next_across = move_y(head, 1), move_y(tail, -1), move_xh(from_next)
    crossed[4] = move_core(stays_across)
    crossed[1] = move_core(after(from_last, crossed[4]))
    last_head, next_tail, next_across, head, tail, from_far, crossed[1], last_across = staged(
        (last_head, next_tail, next_across, head, tail, from_far, crossed[1], last_across)
    )
    last_tail, next_head = move_y(tail, 1), move_y(head, -1)
    far_head, far_tail = move_y(last_head, 1), move_y(next_tail, -1)
    far_across = move_xh(from_far)
    rows = [head, tail, last_head, last_tail, next_head, next_tail, far_head, far_tail]
    pieces = [stays, from_last, from_next, from_far, stays_across, last_across, next_across, far_across]
    crossed[2] = move_core(from_next)
    crossed[5] = move_core(after(last_across, crossed[2]))
    crossed[6] = move_core(after(next_across, crossed[5]))
    crossed[3] = move_core(after(from_far, crossed[6]))
    crossed[7] = move_core(far_across)
    down_across = move_xh(after(down, far_across))
    hidden, rollout_gate_up = first_matmul(where, rows, pieces + [crossed[i] for i in range(8)])

    hiddens = [hidden, move_y(hidden, 1), move_y(hidden, -1), move_y(hidden, 2)]
    downs = [down, down_across]
    downs = downs + [move_core(piece) for piece in downs]
    result = second_matmul(where, hiddens, downs)
    outs, slices = result[:4], result[4:]
    parts = [outs[0]] + [move_y(part, shift) for part, shift in zip(outs[1:], SHIFTS[1:])]
    backs = [move_home(chunk, k) for k, chunk in enumerate(regroup(parts))]
    slices = [slices[0]] + [move_y(part, shift) for part, shift in zip(slices[1:], SHIFTS[1:])]
    rollout_down = place_down(where, slices)
    backs, rollout_down = staged((backs, rollout_down))
    own, other = combine(where, meta, other_meta, backs)
    moe_out = (own + move_core(other)).astype(BF16)
    return (new_master_gate_up, new_master_down, rollout_gate_up, rollout_down, moe_out)


def solution(mesh):
    wide, tall, rows = P("exp", None, None, "ten"), P("exp", None, "ten"), P(("exp", "ten"), None)
    return jax.shard_map(
        body,
        mesh=mesh,
        in_specs=(wide,) * 4 + (tall,) * 4 + (rows,) * 3,
        out_specs=(wide, tall, P("exp", None, "ten", None), P("exp", "ten", None), rows),
        check_vma=False,
    )
```

```python
import functools

import jax
import jax.numpy as jnp
from jax import lax
from jax.experimental import pallas as pl
from jax.experimental.pallas import tpu as pltpu
from jax.sharding import PartitionSpec as P

beta_first = 0.9
beta_second = 0.95
learn_rate = 0.01
weight_decay = 0.1
adam_epsilon = 1e-08
bias_first = 1.0 - 0.9**50
bias_second = 1.0 - 0.95**50

F32 = jnp.float32
BF16 = jnp.bfloat16
VMEM = pl.BlockSpec(memory_space=pltpu.VMEM)
SMEM = pl.BlockSpec(memory_space=pltpu.SMEM)
ANY = pl.BlockSpec(memory_space=pl.ANY)
NT = (((1,), (1,)), ((), ()))

SHIFTS = (0, -1, 1, 2)
AXES = ("xl", "z", "y", "xh", "core")
SLOTS = 12


def adamw_update(master, grads, first, second):
    moment_one = beta_first * first + (1.0 - beta_first) * grads
    moment_two = beta_second * second + (1.0 - beta_second) * grads * grads
    scaled = moment_one * (1.0 / bias_first)
    scaled = scaled / (jnp.sqrt(moment_two * (1.0 / bias_second)) + adam_epsilon)
    return master - learn_rate * (scaled + weight_decay * master)


def params(mib=20):
    return pltpu.CompilerParams(vmem_limit_bytes=mib << 20)


def cost(flops, nbytes):
    return pl.CostEstimate(flops=int(flops), bytes_accessed=int(nbytes), transcendentals=0)


def move(array, target):
    pairs = []
    for i in range(128):
        xl, z, y, xh, core = i // 64, i // 16 % 4, i // 4 % 4, i // 2 % 2, i % 2
        a, b, c, d, f = target(xl, z, y, xh, core)
        pairs.append((i, ((a * 4 + b % 4) * 4 + c % 4) * 4 + d * 2 + f))
    return lax.ppermute(array, AXES, pairs)


def move_y(array, shift):
    return move(array, lambda xl, z, y, xh, core: (xl, z, y + shift, xh, core))


def move_xh(array):
    return move(array, lambda xl, z, y, xh, core: (xl, z, y, 1 - xh, core))


def move_core(array):
    return move(array, lambda xl, z, y, xh, core: (xl, z, y, xh, 1 - core))


def staged(arrays):
    return lax.optimization_barrier(arrays)


def after(arrays, others):
    return lax.optimization_barrier((arrays, others))[0]


def adam_kernel(count, parts, rows, blocks_ref, *refs):
    ins, rest = refs[:4], refs[4:]
    new_ref, pieces = rest[-(count + 5)], rest[-(count + 4) : -4]
    held_ref, made_ref, in_sem, out_sem = rest[-4:]
    steps = [(i, p, q) for i in range(count) for p in range(parts) for q in range(rows // 384)]

    def at(ref, step):
        i, part, q = steps[step]
        start = pl.multiple_of(blocks_ref[i] * rows + q * 384, 384)
        return ref.at[0, part, pl.ds(start, 384)]

    copies = [
        [
            pltpu.make_async_copy(at(ref, step), held_ref.at[step, j], in_sem.at[step, j])
            for j, ref in enumerate(ins)
        ]
        for step in range(len(steps))
    ]
    for step in copies:
        for copy in step:
            copy.start()
    outs = []
    for step, (i, part, q) in enumerate(steps):
        for copy in copies[step]:
            copy.wait()

        def some(r, carry, step=step, i=i, part=part, q=q):
            here = pl.ds(pl.multiple_of(r * 64, 64), 64)
            new = adamw_update(*(held_ref[step, j, here] for j in range(4)))
            made_ref[step, here] = new
            pieces[i][part, pl.ds(pl.multiple_of(q * 384 + r * 64, 64), 64)] = new.astype(BF16)
            return carry

        lax.fori_loop(0, 6, some, 0)
        out = pltpu.make_async_copy(made_ref.at[step], at(new_ref, step), out_sem.at[step])
        out.start()
        outs.append(out)
    for out in outs:
        out.wait()


def adam(blocks, arrays, target, rows):
    count, parts = blocks.shape[0], arrays[0].shape[1]
    steps = count * parts * (rows // 384)
    given = [] if target is None else [target]
    return pl.pallas_call(
        functools.partial(adam_kernel, count, parts, rows),
        in_specs=[SMEM] + [ANY] * (4 + len(given)),
        out_specs=[ANY] + [VMEM] * count,
        out_shape=[jax.ShapeDtypeStruct(arrays[0].shape, F32)]
        + [jax.ShapeDtypeStruct((parts, rows, 256), BF16)] * count,
        scratch_shapes=[
            pltpu.VMEM((steps, 4, 384, 256), F32),
            pltpu.VMEM((steps, 384, 256), F32),
            pltpu.SemaphoreType.DMA((steps, 4)),
            pltpu.SemaphoreType.DMA((steps,)),
        ],
        input_output_aliases={5: 0} if given else {},
        cost_estimate=cost(0, count * parts * rows * 256 * 22),
        compiler_params=params(56),
        name="adam",
    )(blocks, *arrays, *given)


def packed_row(row):
    expert = (row * 2731) >> 16
    rest = row - 24 * expert
    half = (rest >= SLOTS).astype(jnp.int32)
    return expert, half, rest - SLOTS * half


def iota(shape, axis):
    return lax.broadcasted_iota(jnp.int32, shape, axis)


def dispatch_kernel(ids_ref, tokens_ref, out_ref):
    expert = iota((128, 32), 0)
    named = jnp.where((ids_ref[0:1, :] == expert) | (ids_ref[1:2, :] == expert), 1.0, 0.0)
    before = jnp.where(iota((32, 32), 0) < iota((32, 32), 1), 1.0, 0.0).astype(BF16)
    place = jnp.dot(named.astype(BF16), before, preferred_element_type=F32)
    place = jnp.where(named > 0.0, place, 99.0).astype(BF16)
    owner, _, _ = packed_row(iota((192, 128), 0))
    at_expert = jnp.where(owner == iota((192, 128), 1), 1.0, 0.0).astype(BF16)
    found = jnp.dot(at_expert, place, preferred_element_type=F32)
    _, half, slot = packed_row(iota((192, 32), 0))
    hit = found == slot.astype(F32)
    low = jnp.where(hit & (half == 0), 1.0, 0.0).astype(BF16)
    high = jnp.where(hit & (half == 1), 1.0, 0.0).astype(BF16)
    packed = jnp.dot(low, tokens_ref[:, :2048], preferred_element_type=F32)
    packed += jnp.dot(high, tokens_ref[:, 2048:], preferred_element_type=F32)
    for e in range(8):
        out_ref[e] = packed[e * 24 : (e + 1) * 24].astype(BF16)


def dispatch(ids, tokens):
    return pl.pallas_call(
        dispatch_kernel,
        in_specs=[VMEM] * 2,
        out_specs=VMEM,
        out_shape=jax.ShapeDtypeStruct((8, 24, 2048), BF16),
        cost_estimate=cost(2 * 192 * 64 * 2048, 2 << 20),
        compiler_params=params(),
        name="dispatch",
    )(ids, tokens)


def unpack_kernel(where_ref, packed_ref, head_ref, tail_ref):
    packed = jnp.concatenate([packed_ref[e].astype(F32) for e in range(8)], axis=0).astype(BF16)
    expert, half, slot = packed_row(iota((96, 192), 1))
    mine = iota((96, 192), 0) == expert * SLOTS + slot
    for h in range(2):
        taking = jnp.where(mine & (half == h), 1.0, 0.0).astype(BF16)
        rows = jnp.dot(taking, packed, preferred_element_type=F32)
        head_ref[:, h * 2048 : (h + 1) * 2048] = rows[:48].astype(BF16)
        tail_ref[:, h * 2048 : (h + 1) * 2048] = rows[48:].astype(BF16)


def unpack(where, packed):
    return pl.pallas_call(
        unpack_kernel,
        in_specs=[SMEM, VMEM],
        out_specs=[VMEM] * 2,
        out_shape=[jax.ShapeDtypeStruct((48, 4096), BF16)] * 2,
        cost_estimate=cost(4 * 96 * 192 * 2048, 2 << 20),
        compiler_params=params(),
        name="unpack",
    )(where, packed)


def mix_kernel(ids_ref, weights_ref, out_ref):
    expert = iota((128, 32), 0)
    first, second = ids_ref[0:1, :] == expert, ids_ref[1:2, :] == expert
    named = jnp.where(first | second, 1.0, 0.0)
    before = jnp.where(iota((32, 32), 0) < iota((32, 32), 1), 1.0, 0.0).astype(BF16)
    place = jnp.dot(named.astype(BF16), before, preferred_element_type=F32)
    place = jnp.where(named > 0.0, place, 99.0).astype(BF16)
    left = jnp.where(first, weights_ref[0:1, :], 0.0) + jnp.where(second, weights_ref[1:2, :], 0.0)
    owner, _, _ = packed_row(iota((192, 128), 0))
    at_expert = jnp.where(owner == iota((192, 128), 1), 1.0, 0.0).astype(BF16)
    found = jnp.dot(at_expert, place, preferred_element_type=F32)
    _, half, slot = packed_row(iota((192, 32), 0))
    hit = found == slot.astype(F32)
    same = jnp.where(iota((32, 32), 0) == iota((32, 32), 1), 1.0, 0.0).astype(BF16)
    for n in range(3):
        piece = left.astype(BF16)
        left = left - piece.astype(F32)
        spread = jnp.dot(at_expert, piece, preferred_element_type=F32)
        for h in range(2):
            part = jnp.where(hit & (half == h), spread, 0.0).astype(BF16)
            turned = lax.dot_general(same, part, NT, preferred_element_type=F32)
            out_ref[n * 64 + h * 32 : n * 64 + h * 32 + 32, :] = turned.astype(BF16)


def mix(ids, weights):
    return pl.pallas_call(
        mix_kernel,
        in_specs=[VMEM] * 2,
        out_specs=VMEM,
        out_shape=jax.ShapeDtypeStruct((192, 192), BF16),
        cost_estimate=cost(0, 1 << 18),
        compiler_params=params(),
        name="mix",
    )(ids, weights)


def combine_kernel(mixing_ref, back_ref, out_ref):
    for block in range(4):
        back = jnp.concatenate([back_ref[e * 4 + block].astype(F32) for e in range(8)], axis=0)
        mixed = jnp.dot(mixing_ref[...], back.astype(BF16), preferred_element_type=F32)
        for h in range(2):
            part = mixed[h * 32 : h * 32 + 32] + mixed[h * 32 + 64 : h * 32 + 96]
            part += mixed[h * 32 + 128 : h * 32 + 160]
            start = block * 1024 + h * 512
            out_ref[:, start : start + 512] = part.astype(BF16)


def combine(mixing, back):
    return pl.pallas_call(
        combine_kernel,
        in_specs=[VMEM] * 2,
        out_specs=VMEM,
        out_shape=jax.ShapeDtypeStruct((32, 4096), BF16),
        cost_estimate=cost(2 * 192 * 192 * 2048, 2 << 20),
        compiler_params=params(),
        name="combine",
    )(mixing, back)


def wrap(y):
    y = jnp.where(y >= 4, y - 4, y)
    return jnp.where(y < 0, y + 4, y)


PIECES = (((0, 0), (-1, 0), (1, 0), (0, 1)), ((2, 0), (-1, 1), (1, 1)), ((2, 1),))


def piece_columns(where_ref, crossed):
    y, xh, core = where_ref[0], where_ref[1], where_ref[2]
    core = 1 - core if crossed else core
    for f, group in enumerate(PIECES):
        for i, (shift, other) in enumerate(group):
            block = wrap(y + shift) * 4 + (1 - xh if other else xh) * 2 + core
            yield f, i, pl.ds(pl.multiple_of(block * 256, 256), 256)


def half_product(where_ref, x_ref, groups, x_copies, crossed, xc_ref, w_ref, w_sem):
    places = list(piece_columns(where_ref, crossed))
    copies = [
        pltpu.make_async_copy(
            groups[f].at[pl.ds(2 * i, 2)], w_ref.at[:, :, pl.ds(n * 256, 256)], w_sem.at[n]
        )
        for n, (f, i, _) in enumerate(places)
    ]
    for copy in x_copies + copies:
        copy.start()
    for copy in x_copies:
        copy.wait()
    for n, (_, _, columns) in enumerate(places):
        xc_ref[:, n * 256 : n * 256 + 256] = x_ref[:, columns]
    for copy in copies:
        copy.wait()
    return [
        lax.dot_general(xc_ref[...], w_ref[g], NT, preferred_element_type=F32) for g in range(2)
    ]


def first_half_kernel(where_ref, *refs):
    rows, groups = refs[:8], refs[8:11]
    x_ref, acc_ref, xc_ref, w_ref, x_sem, w_sem = refs[11:]
    x_copies = [
        pltpu.make_async_copy(rows[i], x_ref.at[pl.ds(i * 48, 48)], x_sem.at[i]) for i in range(8)
    ]
    products = half_product(where_ref, x_ref, groups, x_copies, False, xc_ref, w_ref, w_sem)
    acc_ref[0], acc_ref[1] = products


def last_half_kernel(where_ref, x_ref, acc_ref, *refs):
    groups, (hidden_ref, xc_ref, w_ref, w_sem) = refs[:3], refs[3:]
    gate, up = half_product(where_ref, x_ref, groups, [], True, xc_ref, w_ref, w_sem)
    gate, up = acc_ref[0] + gate, acc_ref[1] + up
    hidden_ref[...] = (gate / (1.0 + jnp.exp(-gate)) * up).astype(BF16)


HALF_SCRATCH = [pltpu.VMEM((384, 2048), BF16), pltpu.VMEM((2, 384, 2048), BF16)]


def first_half(where, rows, groups):
    return pl.pallas_call(
        first_half_kernel,
        in_specs=[SMEM] + [ANY] * 11,
        out_specs=[VMEM] * 2,
        out_shape=[
            jax.ShapeDtypeStruct((384, 4096), BF16),
            jax.ShapeDtypeStruct((2, 384, 384), F32),
        ],
        scratch_shapes=HALF_SCRATCH
        + [pltpu.SemaphoreType.DMA((8,)), pltpu.SemaphoreType.DMA((8,))],
        cost_estimate=cost(2 * 384 * 768 * 2048, 8 << 20),
        compiler_params=params(36),
        name="first_half",
    )(where, *rows, *groups)


def last_half(where, x, acc, groups):
    return pl.pallas_call(
        last_half_kernel,
        in_specs=[SMEM, VMEM, VMEM] + [ANY] * 3,
        out_specs=VMEM,
        out_shape=jax.ShapeDtypeStruct((384, 384), BF16),
        scratch_shapes=HALF_SCRATCH + [pltpu.SemaphoreType.DMA((8,))],
        cost_estimate=cost(2 * 384 * 768 * 2048, 8 << 20),
        compiler_params=params(),
        name="last_half",
    )(where, x, acc, *groups)


def place_gate_up_kernel(where_ref, *refs):
    groups, out_ref, sem = (refs[:3], refs[3:6]), refs[6], refs[7]
    first = pl.multiple_of((where_ref[1] * 2 + where_ref[2]) * 96, 96)
    copies = []
    for side in range(2):
        for n, (f, i, columns) in enumerate(piece_columns(where_ref, side == 1)):
            copies.append(
                pltpu.make_async_copy(
                    groups[side][f].at[pl.ds(2 * i, 2), pl.ds(first, 96), :],
                    out_ref.at[0, :, :, columns],
                    sem.at[side, n],
                )
            )
    for copy in copies:
        copy.start()
    for copy in copies:
        copy.wait()


def place_gate_up(where, groups):
    return pl.pallas_call(
        place_gate_up_kernel,
        in_specs=[SMEM] + [ANY] * 6,
        out_specs=VMEM,
        out_shape=jax.ShapeDtypeStruct((1, 2, 96, 4096), BF16),
        scratch_shapes=[pltpu.SemaphoreType.DMA((2, 8))],
        cost_estimate=cost(0, 4 << 20),
        compiler_params=params(),
        name="place_gate_up",
    )(where, *groups)


def spread_kernel(where_ref, *refs):
    downs, d_ref, slices, d_sem, out_sem = refs[:4], refs[4], refs[5:9], refs[9], refs[10]
    y, xh, core = where_ref[0], where_ref[1], where_ref[2]
    copies = []
    for side in range(2):
        rest, first = downs[2 * side], downs[2 * side + 1]
        from_core = 1 - core if side else core
        same, other = (
            pl.ds(pl.multiple_of((from_xh * 2 + from_core) * 256, 256), 256)
            for from_xh in (xh, 1 - xh)
        )
        for source, rows, columns in (
            (rest.at[pl.ds(0, 1536)], pl.ds(0, 1536), same),
            (rest.at[pl.ds(1536, 768)], pl.ds(768, 768), other),
            (first.at[2], pl.ds(0, 384), other),
            (first.at[3], pl.ds(384, 384), other),
        ):
            n = len(copies)
            copies.append(pltpu.make_async_copy(source, d_ref.at[rows, columns], d_sem.at[n]))
    for copy in copies:
        copy.start()
    for copy in copies:
        copy.wait()
    sends = []
    for j, shift in enumerate(SHIFTS):
        first = pl.multiple_of((wrap(y + shift) * 4 + xh * 2 + core) * 96, 96)
        send = pltpu.make_async_copy(d_ref.at[pl.ds(first, 96)], slices[j], out_sem.at[j])
        send.start()
        sends.append(send)
    for send in sends:
        send.wait()


def spread_down(where, downs):
    return pl.pallas_call(
        spread_kernel,
        in_specs=[SMEM] + [ANY] * 4,
        out_specs=[VMEM] * 5,
        out_shape=[jax.ShapeDtypeStruct((1536, 1024), BF16)]
        + [jax.ShapeDtypeStruct((96, 1024), BF16)] * 4,
        scratch_shapes=[pltpu.SemaphoreType.DMA((8,)), pltpu.SemaphoreType.DMA((4,))],
        cost_estimate=cost(0, 8 << 20),
        compiler_params=params(),
        name="spread_down",
    )(where, *downs)


def second_kernel(where_ref, *refs):
    hidden, d_ref, sent_ref, h_ref, out_ref, h_sem, out_sem = refs[:5], *refs[5:]
    y = where_ref[0]
    h_copies = []
    for d, shift in enumerate(SHIFTS):
        columns = pl.ds(pl.multiple_of(wrap(y + shift) * 384, 128), 384)
        for g, origin in enumerate(SHIFTS):
            there = [(s - origin + shift) % 4 for s in SHIFTS].index(0)
            h_copies.append(
                pltpu.make_async_copy(
                    hidden[d + there // 2].at[pl.ds(there % 2 * 96, 96)]
                    if d == 3
                    else hidden[d].at[pl.ds(there * 96, 96)],
                    h_ref.at[pl.ds(g * 96, 96), columns],
                    h_sem.at[d * 4 + g],
                )
            )
    for copy in h_copies:
        copy.start()
    for copy in h_copies:
        copy.wait()
    halves = [
        jnp.dot(h_ref[...], d_ref[:, h * 512 : h * 512 + 512], preferred_element_type=F32)
        for h in range(2)
    ]
    halves = [half.astype(BF16) for half in halves]
    expert, half, slot = packed_row(iota((192, 96), 0))
    mine = iota((192, 96), 1) == expert * SLOTS + slot
    packing = [jnp.where(mine & (half == h), 1.0, 0.0).astype(BF16) for h in range(2)]
    for g, shift in enumerate(SHIFTS):
        rows = slice(g * 96, (g + 1) * 96)
        packed = jnp.dot(packing[0], halves[0][rows], preferred_element_type=F32)
        packed += jnp.dot(packing[1], halves[1][rows], preferred_element_type=F32)
        for e in range(8):
            out_ref[e * 4 + wrap(y + shift)] = packed[e * 24 : (e + 1) * 24].astype(BF16)
    send = pltpu.make_async_copy(out_ref, sent_ref, out_sem)
    send.start()
    send.wait()


def second_matmul(where, hidden, down):
    return pl.pallas_call(
        second_kernel,
        in_specs=[SMEM] + [ANY] * 5 + [VMEM],
        out_specs=ANY,
        out_shape=jax.ShapeDtypeStruct((32, 24, 512), BF16),
        scratch_shapes=[
            pltpu.VMEM((384, 1536), BF16),
            pltpu.VMEM((32, 24, 512), BF16),
            pltpu.SemaphoreType.DMA((16,)),
            pltpu.SemaphoreType.DMA,
        ],
        cost_estimate=cost(2 * 384 * 1536 * 1024, 6 << 20),
        compiler_params=params(),
        name="second_matmul",
    )(where, *hidden, down)


def place_kernel(where_ref, *refs):
    parts, out_ref, sem = refs[:4], refs[4], refs[5]
    copies = []
    for j, shift in enumerate(SHIFTS):
        columns = pl.ds(pl.multiple_of(wrap(where_ref[0] - shift) * 1024, 1024), 1024)
        copies.append(pltpu.make_async_copy(parts[j], out_ref.at[0, :, columns], sem.at[j]))
    for copy in copies:
        copy.start()
    for copy in copies:
        copy.wait()


def place_down(where, parts):
    return pl.pallas_call(
        place_kernel,
        in_specs=[SMEM] + [ANY] * 4,
        out_specs=ANY,
        out_shape=jax.ShapeDtypeStruct((1, 96, 4096), BF16),
        scratch_shapes=[pltpu.SemaphoreType.DMA((4,))],
        cost_estimate=cost(0, 2 << 20),
        compiler_params=params(),
        name="place_down",
    )(where, *parts)


def body(
    master_gate_up,
    grad_gate_up,
    first_gate_up,
    second_gate_up,
    master_down,
    grad_down,
    first_down,
    second_down,
    tokens,
    route_ids,
    route_weights,
):
    y, xh, core = lax.axis_index("y"), lax.axis_index("xh"), lax.axis_index("core")
    where = jnp.stack([y, xh, core]).astype(jnp.int32)

    dispatched = dispatch(route_ids.T, tokens)
    packed = lax.all_to_all(dispatched, ("xl", "z"), split_axis=0, concat_axis=0, tiled=True)

    gate_up = (master_gate_up, grad_gate_up, first_gate_up, second_gate_up)
    near = jnp.stack([(y + 1) % 4, (y + 3) % 4, y]).astype(jnp.int32)
    near = after(near, dispatched)
    partial, to_next, to_last, stays = adam(near, gate_up, None, 384)
    from_last, from_next, stays_across = move_y(to_next, 1), move_y(to_last, -1), move_xh(stays)
    far = ((y + 2) % 4).astype(jnp.int32)[None]
    new_master_gate_up, to_far = adam(far, gate_up, partial, 384)

    down_arrays = tuple(a[:, None] for a in (master_down, grad_down, first_down, second_down))
    whole = after(jnp.zeros((1,), jnp.int32), to_far)
    new_master_down, down = adam(whole, down_arrays, None, 1536)
    new_master_down, down = new_master_down[:, 0], down[0]

    from_last, from_next, stays_across, packed, to_far, down = staged(
        (from_last, from_next, stays_across, packed, to_far, down)
    )
    head, tail = unpack(where, packed)
    from_far, last_head, next_tail = move_y(to_far, 2), move_y(head, 1), move_y(tail, -1)
    last_across, next_across = move_xh(from_last), move_xh(from_next)
    first_four = jnp.concatenate([stays, from_last, from_next, stays_across], axis=0)
    from_far, last_head, next_tail, last_across, next_across, down, first_four, head, tail = staged(
        (from_far, last_head, next_tail, last_across, next_across, down, first_four, head, tail)
    )
    far_head, far_tail = move_y(last_head, 1), move_y(next_tail, -1)
    last_tail, next_head = move_y(tail, 1), move_y(head, -1)
    far_across = move_xh(
        jnp.concatenate([from_far, down[:768].reshape(2, 384, 256)], axis=0)
    )
    second_three = jnp.concatenate([from_far, last_across, next_across], axis=0)
    rows = [head, tail, last_head, last_tail, next_head, next_tail, far_head, far_tail]
    rows, groups, down = staged((rows, [first_four, second_three, far_across], down))
    crossed = [move_core(group) for group in groups]
    down_across = move_xh(down[768:])
    mixing = mix(after(route_ids.T, down), route_weights.T)
    hidden = last_half(where, *first_half(where, rows, groups), crossed)

    from_last, from_next = move_y(hidden, 1), move_y(hidden, -1)
    far_first, far_second = move_y(from_last[:192], 1), move_y(from_next[192:], -1)
    hiddens = [hidden, from_last, from_next, far_first, far_second]
    rest = jnp.concatenate(after([down, down_across], hidden), axis=0)
    rest_crossed = move_core(rest)
    downs = [rest, groups[2], rest_crossed, crossed[2]]
    downs, *slices = spread_down(where, downs)
    slices = [slices[0]] + [move_y(part, shift) for part, shift in zip(slices[1:], SHIFTS[1:])]
    rollout_down = place_down(where, slices)
    hiddens, rollout_down = staged((hiddens, rollout_down))
    result = second_matmul(where, hiddens, downs)
    back = lax.all_to_all(result, ("xl", "z", "y"), split_axis=0, concat_axis=0, tiled=True)
    rollout_gate_up = place_gate_up(where, groups + crossed)
    moe_out = combine(mixing, back)
    return (new_master_gate_up, new_master_down, rollout_gate_up, rollout_down, moe_out)


def solution(mesh):
    parts = jax.sharding.Mesh(mesh.devices.reshape(2, 4, 4, 2, 2), AXES)
    exp, ten = ("xl", "z"), ("y", "xh", "core")
    wide, tall, rows = P(exp, None, None, ten), P(exp, None, ten), P(AXES, None)
    return jax.shard_map(
        body,
        mesh=parts,
        in_specs=(wide,) * 4 + (tall,) * 4 + (rows,) * 3,
        out_specs=(wide, tall, P(exp, None, ten, None), P(exp, ten, None), rows),
        check_vma=False,
    )
```

```python
import functools

import jax
import jax.numpy as jnp
from jax import lax
from jax.experimental import pallas as pl
from jax.experimental.pallas import tpu as pltpu
from jax.sharding import PartitionSpec as P

beta_first = 0.9
beta_second = 0.95
learn_rate = 0.01
weight_decay = 0.1
adam_epsilon = 1e-08
bias_first = 1.0 - 0.9**50
bias_second = 1.0 - 0.95**50

F32 = jnp.float32
BF16 = jnp.bfloat16
VMEM = pl.BlockSpec(memory_space=pltpu.VMEM)
SMEM = pl.BlockSpec(memory_space=pltpu.SMEM)
ANY = pl.BlockSpec(memory_space=pl.ANY)
NT = (((1,), (1,)), ((), ()))

SHIFTS = (0, -1, 1, 2)
AXES = ("xl", "z", "y", "xh", "core")
SLOTS = 12


def adamw_update(master, grads, first, second):
    moment_one = beta_first * first + (1.0 - beta_first) * grads
    moment_two = beta_second * second + (1.0 - beta_second) * grads * grads
    scaled = moment_one * (1.0 / bias_first)
    scaled = scaled / (jnp.sqrt(moment_two * (1.0 / bias_second)) + adam_epsilon)
    return master - learn_rate * (scaled + weight_decay * master)


def params(mib=20):
    return pltpu.CompilerParams(vmem_limit_bytes=mib << 20)


def cost(flops, nbytes):
    return pl.CostEstimate(flops=int(flops), bytes_accessed=int(nbytes), transcendentals=0)


def move(array, target):
    pairs = []
    for i in range(128):
        xl, z, y, xh, core = i // 64, i // 16 % 4, i // 4 % 4, i // 2 % 2, i % 2
        a, b, c, d, f = target(xl, z, y, xh, core)
        pairs.append((i, ((a * 4 + b % 4) * 4 + c % 4) * 4 + d * 2 + f))
    return lax.ppermute(array, AXES, pairs)


def move_y(array, shift):
    return move(array, lambda xl, z, y, xh, core: (xl, z, y + shift, xh, core))


def move_xh(array):
    return move(array, lambda xl, z, y, xh, core: (xl, z, y, 1 - xh, core))


def move_core(array):
    return move(array, lambda xl, z, y, xh, core: (xl, z, y, xh, 1 - core))


def staged(arrays):
    return lax.optimization_barrier(arrays)


def after(arrays, others):
    return lax.optimization_barrier((arrays, others))[0]


def adam_kernel(count, parts, rows, blocks_ref, *refs):
    ins, rest = refs[:4], refs[4:]
    new_ref, pieces = rest[-(count + 5)], rest[-(count + 4) : -4]
    held_ref, made_ref, in_sem, out_sem = rest[-4:]
    steps = [(i, p, q) for i in range(count) for p in range(parts) for q in range(rows // 384)]

    def at(ref, step):
        i, part, q = steps[step]
        start = pl.multiple_of(blocks_ref[i] * rows + q * 384, 384)
        return ref.at[0, part, pl.ds(start, 384)]

    copies = [
        [
            pltpu.make_async_copy(at(ref, step), held_ref.at[step, j], in_sem.at[step, j])
            for j, ref in enumerate(ins)
        ]
        for step in range(len(steps))
    ]
    for step in copies:
        for copy in step:
            copy.start()
    outs = []
    for step, (i, part, q) in enumerate(steps):
        for copy in copies[step]:
            copy.wait()

        def some(r, carry, step=step, i=i, part=part, q=q):
            here = pl.ds(pl.multiple_of(r * 64, 64), 64)
            new = adamw_update(*(held_ref[step, j, here] for j in range(4)))
            made_ref[step, here] = new
            pieces[i][part, pl.ds(pl.multiple_of(q * 384 + r * 64, 64), 64)] = new.astype(BF16)
            return carry

        lax.fori_loop(0, 6, some, 0)
        out = pltpu.make_async_copy(made_ref.at[step], at(new_ref, step), out_sem.at[step])
        out.start()
        outs.append(out)
    for out in outs:
        out.wait()


def adam(blocks, arrays, target, rows):
    count, parts = blocks.shape[0], arrays[0].shape[1]
    steps = count * parts * (rows // 384)
    given = [] if target is None else [target]
    return pl.pallas_call(
        functools.partial(adam_kernel, count, parts, rows),
        in_specs=[SMEM] + [ANY] * (4 + len(given)),
        out_specs=[ANY] + [VMEM] * count,
        out_shape=[jax.ShapeDtypeStruct(arrays[0].shape, F32)]
        + [jax.ShapeDtypeStruct((parts, rows, 256), BF16)] * count,
        scratch_shapes=[
            pltpu.VMEM((steps, 4, 384, 256), F32),
            pltpu.VMEM((steps, 384, 256), F32),
            pltpu.SemaphoreType.DMA((steps, 4)),
            pltpu.SemaphoreType.DMA((steps,)),
        ],
        input_output_aliases={5: 0} if given else {},
        cost_estimate=cost(0, count * parts * rows * 256 * 22),
        compiler_params=params(56),
        name="adam",
    )(blocks, *arrays, *given)


def packed_row(row):
    expert = (row * 2731) >> 16
    rest = row - 24 * expert
    half = (rest >= SLOTS).astype(jnp.int32)
    return expert, half, rest - SLOTS * half


def iota(shape, axis):
    return lax.broadcasted_iota(jnp.int32, shape, axis)


def dispatch_kernel(where_ref, near_ref, ids_ref, tokens_ref, out_ref):
    expert = iota((128, 32), 0)
    named = jnp.where((ids_ref[0:1, :] == expert) | (ids_ref[1:2, :] == expert), 1.0, 0.0)
    before = jnp.where(iota((32, 32), 0) < iota((32, 32), 1), 1.0, 0.0).astype(BF16)
    place = jnp.dot(named.astype(BF16), before, preferred_element_type=F32)
    place = jnp.where(named > 0.0, place, 99.0).astype(BF16)
    owner, _, _ = packed_row(iota((192, 128), 0))
    at_expert = jnp.where(owner == iota((192, 128), 1), 1.0, 0.0).astype(BF16)
    found = jnp.dot(at_expert, place, preferred_element_type=F32)
    _, half, slot = packed_row(iota((192, 32), 0))
    hit = found == slot.astype(F32)
    low = jnp.where(hit & (half == 0), 1.0, 0.0).astype(BF16)
    high = jnp.where(hit & (half == 1), 1.0, 0.0).astype(BF16)
    packed = jnp.dot(low, tokens_ref[:, :2048], preferred_element_type=F32)
    packed += jnp.dot(high, tokens_ref[:, 2048:], preferred_element_type=F32)
    for e in range(8):
        out_ref[e] = packed[e * 24 : (e + 1) * 24].astype(BF16)


def dispatch(where, near, ids, tokens):
    return pl.pallas_call(
        dispatch_kernel,
        in_specs=[SMEM] * 2 + [VMEM] * 2,
        out_specs=VMEM,
        out_shape=jax.ShapeDtypeStruct((8, 24, 2048), BF16),
        cost_estimate=cost(2 * 192 * 64 * 2048, 2 << 20),
        compiler_params=params(),
        name="dispatch",
    )(where, near, ids, tokens)


def unpack_kernel(where_ref, packed_ref, head_ref, tail_ref):
    packed = jnp.concatenate([packed_ref[e].astype(F32) for e in range(8)], axis=0).astype(BF16)
    expert, half, slot = packed_row(iota((96, 192), 1))
    mine = iota((96, 192), 0) == expert * SLOTS + slot
    for h in range(2):
        taking = jnp.where(mine & (half == h), 1.0, 0.0).astype(BF16)
        rows = jnp.dot(taking, packed, preferred_element_type=F32)
        head_ref[:, h * 2048 : (h + 1) * 2048] = rows[:48].astype(BF16)
        tail_ref[:, h * 2048 : (h + 1) * 2048] = rows[48:].astype(BF16)


def unpack(where, packed):
    return pl.pallas_call(
        unpack_kernel,
        in_specs=[SMEM, VMEM],
        out_specs=[VMEM] * 2,
        out_shape=[jax.ShapeDtypeStruct((48, 4096), BF16)] * 2,
        cost_estimate=cost(4 * 96 * 192 * 2048, 2 << 20),
        compiler_params=params(),
        name="unpack",
    )(where, packed)


def mix_kernel(ids_ref, weights_ref, out_ref):
    expert = iota((128, 32), 0)
    first, second = ids_ref[0:1, :] == expert, ids_ref[1:2, :] == expert
    named = jnp.where(first | second, 1.0, 0.0)
    before = jnp.where(iota((32, 32), 0) < iota((32, 32), 1), 1.0, 0.0).astype(BF16)
    place = jnp.dot(named.astype(BF16), before, preferred_element_type=F32)
    place = jnp.where(named > 0.0, place, 99.0).astype(BF16)
    left = jnp.where(first, weights_ref[0:1, :], 0.0) + jnp.where(second, weights_ref[1:2, :], 0.0)
    owner, _, _ = packed_row(iota((192, 128), 0))
    at_expert = jnp.where(owner == iota((192, 128), 1), 1.0, 0.0).astype(BF16)
    found = jnp.dot(at_expert, place, preferred_element_type=F32)
    _, half, slot = packed_row(iota((192, 32), 0))
    hit = found == slot.astype(F32)
    same = jnp.where(iota((32, 32), 0) == iota((32, 32), 1), 1.0, 0.0).astype(BF16)
    for n in range(3):
        piece = left.astype(BF16)
        left = left - piece.astype(F32)
        spread = jnp.dot(at_expert, piece, preferred_element_type=F32)
        for h in range(2):
            part = jnp.where(hit & (half == h), spread, 0.0).astype(BF16)
            turned = lax.dot_general(same, part, NT, preferred_element_type=F32)
            out_ref[n * 64 + h * 32 : n * 64 + h * 32 + 32, :] = turned.astype(BF16)


def mix(ids, weights):
    return pl.pallas_call(
        mix_kernel,
        in_specs=[VMEM] * 2,
        out_specs=VMEM,
        out_shape=jax.ShapeDtypeStruct((192, 192), BF16),
        cost_estimate=cost(0, 1 << 18),
        compiler_params=params(),
        name="mix",
    )(ids, weights)


def combine_kernel(mixing_ref, back_ref, out_ref):
    for block in range(4):
        back = jnp.concatenate([back_ref[e * 4 + block].astype(F32) for e in range(8)], axis=0)
        mixed = jnp.dot(mixing_ref[...], back.astype(BF16), preferred_element_type=F32)
        for h in range(2):
            part = mixed[h * 32 : h * 32 + 32] + mixed[h * 32 + 64 : h * 32 + 96]
            part += mixed[h * 32 + 128 : h * 32 + 160]
            start = block * 1024 + h * 512
            out_ref[:, start : start + 512] = part.astype(BF16)


def combine(mixing, back):
    return pl.pallas_call(
        combine_kernel,
        in_specs=[VMEM] * 2,
        out_specs=VMEM,
        out_shape=jax.ShapeDtypeStruct((32, 4096), BF16),
        cost_estimate=cost(2 * 192 * 192 * 2048, 2 << 20),
        compiler_params=params(),
        name="combine",
    )(mixing, back)


def wrap(y):
    y = jnp.where(y >= 4, y - 4, y)
    return jnp.where(y < 0, y + 4, y)


PIECES = (((0, 0), (-1, 0), (1, 0), (0, 1)), ((2, 0), (-1, 1), (1, 1)), ((2, 1),))


def piece_columns(where_ref, crossed):
    y, xh, core = where_ref[0], where_ref[1], where_ref[2]
    core = 1 - core if crossed else core
    for f, group in enumerate(PIECES):
        for i, (shift, other) in enumerate(group):
            block = wrap(y + shift) * 4 + (1 - xh if other else xh) * 2 + core
            yield f, i, pl.ds(pl.multiple_of(block * 256, 256), 256)


def half_product(where_ref, x_ref, groups, x_copies, crossed, xc_ref, w_ref, w_sem):
    places = list(piece_columns(where_ref, crossed))
    copies = [
        pltpu.make_async_copy(
            groups[f].at[pl.ds(2 * i, 2)], w_ref.at[:, :, pl.ds(n * 256, 256)], w_sem.at[n]
        )
        for n, (f, i, _) in enumerate(places)
    ]
    for copy in x_copies + copies:
        copy.start()
    for copy in x_copies:
        copy.wait()
    for n, (_, _, columns) in enumerate(places):
        xc_ref[:, n * 256 : n * 256 + 256] = x_ref[:, columns]
    for copy in copies:
        copy.wait()
    return [
        lax.dot_general(xc_ref[...], w_ref[g], NT, preferred_element_type=F32) for g in range(2)
    ]


def first_half_kernel(where_ref, *refs):
    rows, groups = refs[:8], refs[8:11]
    x_ref, acc_ref, xc_ref, w_ref, x_sem, w_sem = refs[11:]
    x_copies = [
        pltpu.make_async_copy(rows[i], x_ref.at[pl.ds(i * 48, 48)], x_sem.at[i]) for i in range(8)
    ]
    products = half_product(where_ref, x_ref, groups, x_copies, False, xc_ref, w_ref, w_sem)
    acc_ref[0], acc_ref[1] = products


def last_half_kernel(where_ref, x_ref, acc_ref, *refs):
    groups, (hidden_ref, xc_ref, w_ref, w_sem) = refs[:3], refs[3:]
    gate, up = half_product(where_ref, x_ref, groups, [], True, xc_ref, w_ref, w_sem)
    gate, up = acc_ref[0] + gate, acc_ref[1] + up
    hidden_ref[...] = (gate / (1.0 + jnp.exp(-gate)) * up).astype(BF16)


HALF_SCRATCH = [pltpu.VMEM((384, 2048), BF16), pltpu.VMEM((2, 384, 2048), BF16)]


def first_half(where, rows, groups):
    return pl.pallas_call(
        first_half_kernel,
        in_specs=[SMEM] + [ANY] * 11,
        out_specs=[VMEM] * 2,
        out_shape=[
            jax.ShapeDtypeStruct((384, 4096), BF16),
            jax.ShapeDtypeStruct((2, 384, 384), F32),
        ],
        scratch_shapes=HALF_SCRATCH
        + [pltpu.SemaphoreType.DMA((8,)), pltpu.SemaphoreType.DMA((8,))],
        cost_estimate=cost(2 * 384 * 768 * 2048, 8 << 20),
        compiler_params=params(36),
        name="first_half",
    )(where, *rows, *groups)


def last_half(where, x, acc, groups):
    return pl.pallas_call(
        last_half_kernel,
        in_specs=[SMEM, VMEM, VMEM] + [ANY] * 3,
        out_specs=VMEM,
        out_shape=jax.ShapeDtypeStruct((384, 384), BF16),
        scratch_shapes=HALF_SCRATCH + [pltpu.SemaphoreType.DMA((8,))],
        cost_estimate=cost(2 * 384 * 768 * 2048, 8 << 20),
        compiler_params=params(),
        name="last_half",
    )(where, x, acc, *groups)


def place_gate_up_kernel(where_ref, *refs):
    groups, out_ref, sem = (refs[:3], refs[3:6]), refs[6], refs[7]
    first = pl.multiple_of((where_ref[1] * 2 + where_ref[2]) * 96, 96)
    copies = []
    for side in range(2):
        for n, (f, i, columns) in enumerate(piece_columns(where_ref, side == 1)):
            copies.append(
                pltpu.make_async_copy(
                    groups[side][f].at[pl.ds(2 * i, 2), pl.ds(first, 96), :],
                    out_ref.at[0, :, :, columns],
                    sem.at[side, n],
                )
            )
    for copy in copies:
        copy.start()
    for copy in copies:
        copy.wait()


def place_gate_up(where, groups):
    return pl.pallas_call(
        place_gate_up_kernel,
        in_specs=[SMEM] + [ANY] * 6,
        out_specs=VMEM,
        out_shape=jax.ShapeDtypeStruct((1, 2, 96, 4096), BF16),
        scratch_shapes=[pltpu.SemaphoreType.DMA((2, 8))],
        cost_estimate=cost(0, 4 << 20),
        compiler_params=params(),
        name="place_gate_up",
    )(where, *groups)


def spread_kernel(where_ref, *refs):
    downs, d_ref, slices, d_sem, out_sem = refs[:4], refs[4], refs[5:9], refs[9], refs[10]
    y, xh, core = where_ref[0], where_ref[1], where_ref[2]
    copies = []
    for side in range(2):
        rest, first = downs[2 * side], downs[2 * side + 1]
        from_core = 1 - core if side else core
        same, other = (
            pl.ds(pl.multiple_of((from_xh * 2 + from_core) * 256, 256), 256)
            for from_xh in (xh, 1 - xh)
        )
        for source, rows, columns in (
            (rest.at[pl.ds(0, 1536)], pl.ds(0, 1536), same),
            (rest.at[pl.ds(1536, 768)], pl.ds(768, 768), other),
            (first.at[2], pl.ds(0, 384), other),
            (first.at[3], pl.ds(384, 384), other),
        ):
            n = len(copies)
            copies.append(pltpu.make_async_copy(source, d_ref.at[rows, columns], d_sem.at[n]))
    for copy in copies:
        copy.start()
    for copy in copies:
        copy.wait()
    sends = []
    for j, shift in enumerate(SHIFTS):
        first = pl.multiple_of((wrap(y + shift) * 4 + xh * 2 + core) * 96, 96)
        send = pltpu.make_async_copy(d_ref.at[pl.ds(first, 96)], slices[j], out_sem.at[j])
        send.start()
        sends.append(send)
    for send in sends:
        send.wait()


def spread_down(where, downs):
    return pl.pallas_call(
        spread_kernel,
        in_specs=[SMEM] + [ANY] * 4,
        out_specs=[VMEM] * 5,
        out_shape=[jax.ShapeDtypeStruct((1536, 1024), BF16)]
        + [jax.ShapeDtypeStruct((96, 1024), BF16)] * 4,
        scratch_shapes=[pltpu.SemaphoreType.DMA((8,)), pltpu.SemaphoreType.DMA((4,))],
        cost_estimate=cost(0, 8 << 20),
        compiler_params=params(),
        name="spread_down",
    )(where, *downs)


def second_kernel(where_ref, *refs):
    hidden, d_ref, sent_ref, h_ref, out_ref, h_sem, out_sem = refs[:5], *refs[5:]
    y = where_ref[0]
    h_copies = []
    for d, shift in enumerate(SHIFTS):
        columns = pl.ds(pl.multiple_of(wrap(y + shift) * 384, 128), 384)
        for g, origin in enumerate(SHIFTS):
            there = [(s - origin + shift) % 4 for s in SHIFTS].index(0)
            h_copies.append(
                pltpu.make_async_copy(
                    hidden[d + there // 2].at[pl.ds(there % 2 * 96, 96)]
                    if d == 3
                    else hidden[d].at[pl.ds(there * 96, 96)],
                    h_ref.at[pl.ds(g * 96, 96), columns],
                    h_sem.at[d * 4 + g],
                )
            )
    for copy in h_copies:
        copy.start()
    for copy in h_copies:
        copy.wait()
    halves = [
        jnp.dot(h_ref[...], d_ref[:, h * 512 : h * 512 + 512], preferred_element_type=F32)
        for h in range(2)
    ]
    halves = [half.astype(BF16) for half in halves]
    expert, half, slot = packed_row(iota((192, 96), 0))
    mine = iota((192, 96), 1) == expert * SLOTS + slot
    packing = [jnp.where(mine & (half == h), 1.0, 0.0).astype(BF16) for h in range(2)]
    for g, shift in enumerate(SHIFTS):
        rows = slice(g * 96, (g + 1) * 96)
        packed = jnp.dot(packing[0], halves[0][rows], preferred_element_type=F32)
        packed += jnp.dot(packing[1], halves[1][rows], preferred_element_type=F32)
        for e in range(8):
            out_ref[e * 4 + wrap(y + shift)] = packed[e * 24 : (e + 1) * 24].astype(BF16)
    send = pltpu.make_async_copy(out_ref, sent_ref, out_sem)
    send.start()
    send.wait()


def second_matmul(where, hidden, down):
    return pl.pallas_call(
        second_kernel,
        in_specs=[SMEM] + [ANY] * 5 + [VMEM],
        out_specs=ANY,
        out_shape=jax.ShapeDtypeStruct((32, 24, 512), BF16),
        scratch_shapes=[
            pltpu.VMEM((384, 1536), BF16),
            pltpu.VMEM((32, 24, 512), BF16),
            pltpu.SemaphoreType.DMA((16,)),
            pltpu.SemaphoreType.DMA,
        ],
        cost_estimate=cost(2 * 384 * 1536 * 1024, 6 << 20),
        compiler_params=params(),
        name="second_matmul",
    )(where, *hidden, down)


def place_kernel(where_ref, *refs):
    parts, out_ref, sem = refs[:4], refs[4], refs[5]
    copies = []
    for j, shift in enumerate(SHIFTS):
        columns = pl.ds(pl.multiple_of(wrap(where_ref[0] - shift) * 1024, 1024), 1024)
        copies.append(pltpu.make_async_copy(parts[j], out_ref.at[0, :, columns], sem.at[j]))
    for copy in copies:
        copy.start()
    for copy in copies:
        copy.wait()


def place_down(where, parts):
    return pl.pallas_call(
        place_kernel,
        in_specs=[SMEM] + [ANY] * 4,
        out_specs=ANY,
        out_shape=jax.ShapeDtypeStruct((1, 96, 4096), BF16),
        scratch_shapes=[pltpu.SemaphoreType.DMA((4,))],
        cost_estimate=cost(0, 2 << 20),
        compiler_params=params(56),
        name="place_down",
    )(where, *parts)


def body(
    master_gate_up,
    grad_gate_up,
    first_gate_up,
    second_gate_up,
    master_down,
    grad_down,
    first_down,
    second_down,
    tokens,
    route_ids,
    route_weights,
):
    y, xh, core = lax.axis_index("y"), lax.axis_index("xh"), lax.axis_index("core")
    where = jnp.stack([y, xh, core]).astype(jnp.int32)

    near = jnp.stack([(y + 1) % 4, (y + 3) % 4, y]).astype(jnp.int32)
    dispatched = dispatch(where, near, route_ids.T, tokens)
    packed = lax.all_to_all(dispatched, ("xl", "z"), split_axis=0, concat_axis=0, tiled=True)

    gate_up = (master_gate_up, grad_gate_up, first_gate_up, second_gate_up)
    near = after(near, dispatched)
    partial, to_next, to_last, stays = adam(near, gate_up, None, 384)
    from_last, from_next, stays_across = move_y(to_next, 1), move_y(to_last, -1), move_xh(stays)
    far = ((y + 2) % 4).astype(jnp.int32)[None]
    new_master_gate_up, to_far = adam(far, gate_up, partial, 384)

    down_arrays = tuple(a[:, None] for a in (master_down, grad_down, first_down, second_down))
    whole = after(jnp.zeros((1,), jnp.int32), to_far)
    new_master_down, down = adam(whole, down_arrays, None, 1536)
    new_master_down, down = new_master_down[:, 0], down[0]

    from_last, from_next, stays_across, packed, to_far, down = staged(
        (from_last, from_next, stays_across, packed, to_far, down)
    )
    head, tail = unpack(where, packed)
    from_far, last_head, next_tail = move_y(to_far, 2), move_y(head, 1), move_y(tail, -1)
    last_across, next_across = move_xh(from_last), move_xh(from_next)
    first_four = jnp.concatenate([stays, from_last, from_next, stays_across], axis=0)
    from_far, last_head, next_tail, last_across, next_across, down, first_four, head, tail = staged(
        (from_far, last_head, next_tail, last_across, next_across, down, first_four, head, tail)
    )
    far_head, far_tail = move_y(last_head, 1), move_y(next_tail, -1)
    last_tail, next_head = move_y(tail, 1), move_y(head, -1)
    far_across = move_xh(
        jnp.concatenate([from_far, down[:768].reshape(2, 384, 256)], axis=0)
    )
    second_three = jnp.concatenate([from_far, last_across, next_across], axis=0)
    rows = [head, tail, last_head, last_tail, next_head, next_tail, far_head, far_tail]
    rows, groups, down = staged((rows, [first_four, second_three, far_across], down))
    crossed = [move_core(group) for group in groups]
    down_across = move_xh(down[768:])
    mixing = mix(after(route_ids.T, down), route_weights.T)
    hidden = last_half(where, *first_half(where, rows, groups), crossed)

    from_last, from_next = move_y(hidden, 1), move_y(hidden, -1)
    far_first, far_second = move_y(from_last[:192], 1), move_y(from_next[192:], -1)
    hiddens = [hidden, from_last, from_next, far_first, far_second]
    rest = jnp.concatenate(after([down, down_across], hidden), axis=0)
    rest_crossed = move_core(rest)
    downs = [rest, groups[2], rest_crossed, crossed[2]]
    downs, *slices = spread_down(where, downs)
    slices = [slices[0]] + [move_y(part, shift) for part, shift in zip(slices[1:], SHIFTS[1:])]
    hiddens, slices = staged((hiddens, slices))
    result = second_matmul(where, hiddens, downs)
    back = lax.all_to_all(result, ("xl", "z", "y"), split_axis=0, concat_axis=0, tiled=True)
    rollout_down = place_down(where, after(slices, result))
    rollout_gate_up = place_gate_up(where, groups + crossed)
    moe_out = combine(mixing, back)
    return (new_master_gate_up, new_master_down, rollout_gate_up, rollout_down, moe_out)


def solution(mesh):
    parts = jax.sharding.Mesh(mesh.devices.reshape(2, 4, 4, 2, 2), AXES)
    exp, ten = ("xl", "z"), ("y", "xh", "core")
    wide, tall, rows = P(exp, None, None, ten), P(exp, None, ten), P(AXES, None)
    return jax.shard_map(
        body,
        mesh=parts,
        in_specs=(wide,) * 4 + (tall,) * 4 + (rows,) * 3,
        out_specs=(wide, tall, P(exp, None, ten, None), P(exp, ten, None), rows),
        check_vma=False,
    )
```

```python
import functools

import jax
import jax.numpy as jnp
from jax import lax
from jax.experimental import pallas as pl
from jax.experimental.pallas import tpu as pltpu
from jax.sharding import PartitionSpec as P

beta_first = 0.9
beta_second = 0.95
learn_rate = 0.01
weight_decay = 0.1
adam_epsilon = 1e-08
bias_first = 1.0 - 0.9**50
bias_second = 1.0 - 0.95**50

F32 = jnp.float32
BF16 = jnp.bfloat16
VMEM = pl.BlockSpec(memory_space=pltpu.VMEM)
SMEM = pl.BlockSpec(memory_space=pltpu.SMEM)
ANY = pl.BlockSpec(memory_space=pl.ANY)
NT = (((1,), (1,)), ((), ()))

SHIFTS = (0, -1, 1, 2)
AXES = ("xl", "z", "y", "xh", "core")
SLOTS = 12


def adamw_update(master, grads, first, second):
    moment_one = beta_first * first + (1.0 - beta_first) * grads
    moment_two = beta_second * second + (1.0 - beta_second) * grads * grads
    scaled = moment_one * (1.0 / bias_first)
    scaled = scaled / (jnp.sqrt(moment_two * (1.0 / bias_second)) + adam_epsilon)
    return master - learn_rate * (scaled + weight_decay * master)


def params(mib=20):
    return pltpu.CompilerParams(vmem_limit_bytes=mib << 20)


def cost(flops, nbytes):
    return pl.CostEstimate(flops=int(flops), bytes_accessed=int(nbytes), transcendentals=0)


def move(array, target):
    pairs = []
    for i in range(128):
        xl, z, y, xh, core = i // 64, i // 16 % 4, i // 4 % 4, i // 2 % 2, i % 2
        a, b, c, d, f = target(xl, z, y, xh, core)
        pairs.append((i, ((a * 4 + b % 4) * 4 + c % 4) * 4 + d * 2 + f))
    return lax.ppermute(array, AXES, pairs)


def move_y(array, shift):
    return move(array, lambda xl, z, y, xh, core: (xl, z, y + shift, xh, core))


def move_xh(array):
    return move(array, lambda xl, z, y, xh, core: (xl, z, y, 1 - xh, core))


def move_core(array):
    return move(array, lambda xl, z, y, xh, core: (xl, z, y, xh, 1 - core))


def staged(arrays):
    return lax.optimization_barrier(arrays)


def after(arrays, others):
    return lax.optimization_barrier((arrays, others))[0]


def adam_kernel(count, parts, rows, blocks_ref, *refs):
    ins, rest = refs[:4], refs[4:]
    new_ref, pieces = rest[-(count + 5)], rest[-(count + 4) : -4]
    held_ref, made_ref, in_sem, out_sem = rest[-4:]
    steps = [(i, p, q) for i in range(count) for p in range(parts) for q in range(rows // 384)]

    def at(ref, step):
        i, part, q = steps[step]
        start = pl.multiple_of(blocks_ref[i] * rows + q * 384, 384)
        return ref.at[0, part, pl.ds(start, 384)]

    copies = [
        [
            pltpu.make_async_copy(at(ref, step), held_ref.at[step, j], in_sem.at[step, j])
            for j, ref in enumerate(ins)
        ]
        for step in range(len(steps))
    ]
    for step in copies:
        for copy in step:
            copy.start()
    outs = []
    for step, (i, part, q) in enumerate(steps):
        for copy in copies[step]:
            copy.wait()

        def some(r, carry, step=step, i=i, part=part, q=q):
            here = pl.ds(pl.multiple_of(r * 64, 64), 64)
            new = adamw_update(*(held_ref[step, j, here] for j in range(4)))
            made_ref[step, here] = new
            pieces[i][part, pl.ds(pl.multiple_of(q * 384 + r * 64, 64), 64)] = new.astype(BF16)
            return carry

        lax.fori_loop(0, 6, some, 0)
        out = pltpu.make_async_copy(made_ref.at[step], at(new_ref, step), out_sem.at[step])
        out.start()
        outs.append(out)
    for out in outs:
        out.wait()


def adam(blocks, arrays, target, rows):
    count, parts = blocks.shape[0], arrays[0].shape[1]
    steps = count * parts * (rows // 384)
    given = [] if target is None else [target]
    return pl.pallas_call(
        functools.partial(adam_kernel, count, parts, rows),
        in_specs=[SMEM] + [ANY] * (4 + len(given)),
        out_specs=[ANY] + [VMEM] * count,
        out_shape=[jax.ShapeDtypeStruct(arrays[0].shape, F32)]
        + [jax.ShapeDtypeStruct((parts, rows, 256), BF16)] * count,
        scratch_shapes=[
            pltpu.VMEM((steps, 4, 384, 256), F32),
            pltpu.VMEM((steps, 384, 256), F32),
            pltpu.SemaphoreType.DMA((steps, 4)),
            pltpu.SemaphoreType.DMA((steps,)),
        ],
        input_output_aliases={5: 0} if given else {},
        cost_estimate=cost(0, count * parts * rows * 256 * 22),
        compiler_params=params(56),
        name="adam",
    )(blocks, *arrays, *given)


def packed_row(row):
    expert = (row * 2731) >> 16
    rest = row - 24 * expert
    half = (rest >= SLOTS).astype(jnp.int32)
    return expert, half, rest - SLOTS * half


def iota(shape, axis):
    return lax.broadcasted_iota(jnp.int32, shape, axis)


def dispatch_kernel(where_ref, near_ref, ids_ref, tokens_ref, out_ref):
    expert = iota((128, 32), 0)
    named = jnp.where((ids_ref[0:1, :] == expert) | (ids_ref[1:2, :] == expert), 1.0, 0.0)
    before = jnp.where(iota((32, 32), 0) < iota((32, 32), 1), 1.0, 0.0).astype(BF16)
    place = jnp.dot(named.astype(BF16), before, preferred_element_type=F32)
    place = jnp.where(named > 0.0, place, 99.0).astype(BF16)
    owner, _, _ = packed_row(iota((192, 128), 0))
    at_expert = jnp.where(owner == iota((192, 128), 1), 1.0, 0.0).astype(BF16)
    found = jnp.dot(at_expert, place, preferred_element_type=F32)
    _, half, slot = packed_row(iota((192, 32), 0))
    hit = found == slot.astype(F32)
    low = jnp.where(hit & (half == 0), 1.0, 0.0).astype(BF16)
    high = jnp.where(hit & (half == 1), 1.0, 0.0).astype(BF16)
    packed = jnp.dot(low, tokens_ref[:, :2048], preferred_element_type=F32)
    packed += jnp.dot(high, tokens_ref[:, 2048:], preferred_element_type=F32)
    for e in range(8):
        out_ref[e] = packed[e * 24 : (e + 1) * 24].astype(BF16)


def dispatch(where, near, ids, tokens):
    return pl.pallas_call(
        dispatch_kernel,
        in_specs=[SMEM] * 2 + [VMEM] * 2,
        out_specs=VMEM,
        out_shape=jax.ShapeDtypeStruct((8, 24, 2048), BF16),
        cost_estimate=cost(2 * 192 * 64 * 2048, 2 << 20),
        compiler_params=params(),
        name="dispatch",
    )(where, near, ids, tokens)


def unpack_kernel(where_ref, packed_ref, head_ref, tail_ref):
    packed = jnp.concatenate([packed_ref[e].astype(F32) for e in range(8)], axis=0).astype(BF16)
    expert, half, slot = packed_row(iota((96, 192), 1))
    mine = iota((96, 192), 0) == expert * SLOTS + slot
    for h in range(2):
        taking = jnp.where(mine & (half == h), 1.0, 0.0).astype(BF16)
        rows = jnp.dot(taking, packed, preferred_element_type=F32)
        head_ref[:, h * 2048 : (h + 1) * 2048] = rows[:48].astype(BF16)
        tail_ref[:, h * 2048 : (h + 1) * 2048] = rows[48:].astype(BF16)


def unpack(where, packed):
    return pl.pallas_call(
        unpack_kernel,
        in_specs=[SMEM, VMEM],
        out_specs=[VMEM] * 2,
        out_shape=[jax.ShapeDtypeStruct((48, 4096), BF16)] * 2,
        cost_estimate=cost(4 * 96 * 192 * 2048, 2 << 20),
        compiler_params=params(),
        name="unpack",
    )(where, packed)


def mix_kernel(ids_ref, weights_ref, out_ref):
    expert = iota((128, 32), 0)
    first, second = ids_ref[0:1, :] == expert, ids_ref[1:2, :] == expert
    named = jnp.where(first | second, 1.0, 0.0)
    before = jnp.where(iota((32, 32), 0) < iota((32, 32), 1), 1.0, 0.0).astype(BF16)
    place = jnp.dot(named.astype(BF16), before, preferred_element_type=F32)
    place = jnp.where(named > 0.0, place, 99.0).astype(BF16)
    left = jnp.where(first, weights_ref[0:1, :], 0.0) + jnp.where(second, weights_ref[1:2, :], 0.0)
    owner, _, _ = packed_row(iota((192, 128), 0))
    at_expert = jnp.where(owner == iota((192, 128), 1), 1.0, 0.0).astype(BF16)
    found = jnp.dot(at_expert, place, preferred_element_type=F32)
    _, half, slot = packed_row(iota((192, 32), 0))
    hit = found == slot.astype(F32)
    same = jnp.where(iota((32, 32), 0) == iota((32, 32), 1), 1.0, 0.0).astype(BF16)
    for n in range(3):
        piece = left.astype(BF16)
        left = left - piece.astype(F32)
        spread = jnp.dot(at_expert, piece, preferred_element_type=F32)
        for h in range(2):
            part = jnp.where(hit & (half == h), spread, 0.0).astype(BF16)
            turned = lax.dot_general(same, part, NT, preferred_element_type=F32)
            out_ref[n * 64 + h * 32 : n * 64 + h * 32 + 32, :] = turned.astype(BF16)


def mix(ids, weights):
    return pl.pallas_call(
        mix_kernel,
        in_specs=[VMEM] * 2,
        out_specs=VMEM,
        out_shape=jax.ShapeDtypeStruct((192, 192), BF16),
        cost_estimate=cost(0, 1 << 18),
        compiler_params=params(),
        name="mix",
    )(ids, weights)


def combine_kernel(mixing_ref, back_ref, out_ref):
    for block in range(4):
        back = jnp.concatenate([back_ref[e * 4 + block].astype(F32) for e in range(8)], axis=0)
        mixed = jnp.dot(mixing_ref[...], back.astype(BF16), preferred_element_type=F32)
        for h in range(2):
            part = mixed[h * 32 : h * 32 + 32] + mixed[h * 32 + 64 : h * 32 + 96]
            part += mixed[h * 32 + 128 : h * 32 + 160]
            start = block * 1024 + h * 512
            out_ref[:, start : start + 512] = part.astype(BF16)


def combine(mixing, back):
    return pl.pallas_call(
        combine_kernel,
        in_specs=[VMEM] * 2,
        out_specs=VMEM,
        out_shape=jax.ShapeDtypeStruct((32, 4096), BF16),
        cost_estimate=cost(2 * 192 * 192 * 2048, 2 << 20),
        compiler_params=params(),
        name="combine",
    )(mixing, back)


def wrap(y):
    y = jnp.where(y >= 4, y - 4, y)
    return jnp.where(y < 0, y + 4, y)


PIECES = (((0, 0), (-1, 0), (1, 0), (0, 1)), ((2, 0), (-1, 1), (1, 1)), ((2, 1),))


def piece_columns(where_ref, crossed):
    y, xh, core = where_ref[0], where_ref[1], where_ref[2]
    core = 1 - core if crossed else core
    for f, group in enumerate(PIECES):
        for i, (shift, other) in enumerate(group):
            block = wrap(y + shift) * 4 + (1 - xh if other else xh) * 2 + core
            yield f, i, pl.ds(pl.multiple_of(block * 256, 256), 256)


def half_product(where_ref, x_ref, groups, x_copies, crossed, xc_ref, w_ref, w_sem):
    places = list(piece_columns(where_ref, crossed))
    copies = [
        pltpu.make_async_copy(
            groups[f].at[pl.ds(2 * i, 2)], w_ref.at[:, :, pl.ds(n * 256, 256)], w_sem.at[n]
        )
        for n, (f, i, _) in enumerate(places)
    ]
    for copy in x_copies + copies:
        copy.start()
    for copy in x_copies:
        copy.wait()
    for n, (_, _, columns) in enumerate(places):
        xc_ref[:, n * 256 : n * 256 + 256] = x_ref[:, columns]
    for copy in copies:
        copy.wait()
    return [
        lax.dot_general(xc_ref[...], w_ref[g], NT, preferred_element_type=F32) for g in range(2)
    ]


def first_half_kernel(where_ref, *refs):
    rows, groups = refs[:8], refs[8:11]
    x_ref, acc_ref, xc_ref, w_ref, x_sem, w_sem = refs[11:]
    x_copies = [
        pltpu.make_async_copy(rows[i], x_ref.at[pl.ds(i * 48, 48)], x_sem.at[i]) for i in range(8)
    ]
    products = half_product(where_ref, x_ref, groups, x_copies, False, xc_ref, w_ref, w_sem)
    acc_ref[0], acc_ref[1] = products


def last_half_kernel(where_ref, x_ref, acc_ref, *refs):
    groups, (hidden_ref, xc_ref, w_ref, w_sem) = refs[:3], refs[3:]
    gate, up = half_product(where_ref, x_ref, groups, [], True, xc_ref, w_ref, w_sem)
    gate, up = acc_ref[0] + gate, acc_ref[1] + up
    hidden_ref[...] = (gate / (1.0 + jnp.exp(-gate)) * up).astype(BF16)


HALF_SCRATCH = [pltpu.VMEM((384, 2048), BF16), pltpu.VMEM((2, 384, 2048), BF16)]


def first_half(where, rows, groups):
    return pl.pallas_call(
        first_half_kernel,
        in_specs=[SMEM] + [ANY] * 11,
        out_specs=[VMEM] * 2,
        out_shape=[
            jax.ShapeDtypeStruct((384, 4096), BF16),
            jax.ShapeDtypeStruct((2, 384, 384), F32),
        ],
        scratch_shapes=HALF_SCRATCH
        + [pltpu.SemaphoreType.DMA((8,)), pltpu.SemaphoreType.DMA((8,))],
        cost_estimate=cost(2 * 384 * 768 * 2048, 8 << 20),
        compiler_params=params(36),
        name="first_half",
    )(where, *rows, *groups)


def last_half(where, x, acc, groups):
    return pl.pallas_call(
        last_half_kernel,
        in_specs=[SMEM, VMEM, VMEM] + [ANY] * 3,
        out_specs=VMEM,
        out_shape=jax.ShapeDtypeStruct((384, 384), BF16),
        scratch_shapes=HALF_SCRATCH + [pltpu.SemaphoreType.DMA((8,))],
        cost_estimate=cost(2 * 384 * 768 * 2048, 8 << 20),
        compiler_params=params(),
        name="last_half",
    )(where, x, acc, *groups)


def place_gate_up_kernel(where_ref, *refs):
    groups, out_ref, sem = (refs[:3], refs[3:6]), refs[6], refs[7]
    first = pl.multiple_of((where_ref[1] * 2 + where_ref[2]) * 96, 96)
    copies = []
    for side in range(2):
        for n, (f, i, columns) in enumerate(piece_columns(where_ref, side == 1)):
            copies.append(
                pltpu.make_async_copy(
                    groups[side][f].at[pl.ds(2 * i, 2), pl.ds(first, 96), :],
                    out_ref.at[0, :, :, columns],
                    sem.at[side, n],
                )
            )
    for copy in copies:
        copy.start()
    for copy in copies:
        copy.wait()


def place_gate_up(where, groups):
    return pl.pallas_call(
        place_gate_up_kernel,
        in_specs=[SMEM] + [ANY] * 6,
        out_specs=VMEM,
        out_shape=jax.ShapeDtypeStruct((1, 2, 96, 4096), BF16),
        scratch_shapes=[pltpu.SemaphoreType.DMA((2, 8))],
        cost_estimate=cost(0, 4 << 20),
        compiler_params=params(),
        name="place_gate_up",
    )(where, *groups)


def spread_kernel(where_ref, *refs):
    downs, d_ref, slices, d_sem, out_sem = refs[:4], refs[4], refs[5:9], refs[9], refs[10]
    y, xh, core = where_ref[0], where_ref[1], where_ref[2]
    copies = []
    for side in range(2):
        rest, first = downs[2 * side], downs[2 * side + 1]
        from_core = 1 - core if side else core
        same, other = (
            pl.ds(pl.multiple_of((from_xh * 2 + from_core) * 256, 256), 256)
            for from_xh in (xh, 1 - xh)
        )
        for source, rows, columns in (
            (rest.at[pl.ds(0, 1536)], pl.ds(0, 1536), same),
            (rest.at[pl.ds(1536, 768)], pl.ds(768, 768), other),
            (first.at[2], pl.ds(0, 384), other),
            (first.at[3], pl.ds(384, 384), other),
        ):
            n = len(copies)
            copies.append(pltpu.make_async_copy(source, d_ref.at[rows, columns], d_sem.at[n]))
    for copy in copies:
        copy.start()
    for copy in copies:
        copy.wait()
    sends = []
    for j, shift in enumerate(SHIFTS):
        first = pl.multiple_of((wrap(y + shift) * 4 + xh * 2 + core) * 96, 96)
        send = pltpu.make_async_copy(d_ref.at[pl.ds(first, 96)], slices[j], out_sem.at[j])
        send.start()
        sends.append(send)
    for send in sends:
        send.wait()


def spread_down(where, downs):
    return pl.pallas_call(
        spread_kernel,
        in_specs=[SMEM] + [ANY] * 4,
        out_specs=[VMEM] * 5,
        out_shape=[jax.ShapeDtypeStruct((1536, 1024), BF16)]
        + [jax.ShapeDtypeStruct((96, 1024), BF16)] * 4,
        scratch_shapes=[pltpu.SemaphoreType.DMA((8,)), pltpu.SemaphoreType.DMA((4,))],
        cost_estimate=cost(0, 8 << 20),
        compiler_params=params(),
        name="spread_down",
    )(where, *downs)


def second_kernel(where_ref, *refs):
    hidden, d_ref, sent_ref, h_ref, out_ref, h_sem, out_sem = refs[:5], *refs[5:]
    y = where_ref[0]
    h_copies = []
    for d, shift in enumerate(SHIFTS):
        columns = pl.ds(pl.multiple_of(wrap(y + shift) * 384, 128), 384)
        for g, origin in enumerate(SHIFTS):
            there = [(s - origin + shift) % 4 for s in SHIFTS].index(0)
            h_copies.append(
                pltpu.make_async_copy(
                    hidden[d + there // 2].at[pl.ds(there % 2 * 96, 96)]
                    if d == 3
                    else hidden[d].at[pl.ds(there * 96, 96)],
                    h_ref.at[pl.ds(g * 96, 96), columns],
                    h_sem.at[d * 4 + g],
                )
            )
    for copy in h_copies:
        copy.start()
    for copy in h_copies:
        copy.wait()
    halves = [
        jnp.dot(h_ref[...], d_ref[:, h * 512 : h * 512 + 512], preferred_element_type=F32)
        for h in range(2)
    ]
    halves = [half.astype(BF16) for half in halves]
    expert, half, slot = packed_row(iota((192, 96), 0))
    mine = iota((192, 96), 1) == expert * SLOTS + slot
    packing = [jnp.where(mine & (half == h), 1.0, 0.0).astype(BF16) for h in range(2)]
    for g, shift in enumerate(SHIFTS):
        rows = slice(g * 96, (g + 1) * 96)
        packed = jnp.dot(packing[0], halves[0][rows], preferred_element_type=F32)
        packed += jnp.dot(packing[1], halves[1][rows], preferred_element_type=F32)
        for e in range(8):
            out_ref[e * 4 + wrap(y + shift)] = packed[e * 24 : (e + 1) * 24].astype(BF16)
    send = pltpu.make_async_copy(out_ref, sent_ref, out_sem)
    send.start()
    send.wait()


def second_matmul(where, hidden, down):
    return pl.pallas_call(
        second_kernel,
        in_specs=[SMEM] + [ANY] * 5 + [VMEM],
        out_specs=ANY,
        out_shape=jax.ShapeDtypeStruct((32, 24, 512), BF16),
        scratch_shapes=[
            pltpu.VMEM((384, 1536), BF16),
            pltpu.VMEM((32, 24, 512), BF16),
            pltpu.SemaphoreType.DMA((16,)),
            pltpu.SemaphoreType.DMA,
        ],
        cost_estimate=cost(2 * 384 * 1536 * 1024, 6 << 20),
        compiler_params=params(),
        name="second_matmul",
    )(where, *hidden, down)


def place_kernel(where_ref, *refs):
    parts, out_ref, sem = refs[:4], refs[4], refs[5]
    copies = []
    for j, shift in enumerate(SHIFTS):
        columns = pl.ds(pl.multiple_of(wrap(where_ref[0] - shift) * 1024, 1024), 1024)
        copies.append(pltpu.make_async_copy(parts[j], out_ref.at[0, :, columns], sem.at[j]))
    for copy in copies:
        copy.start()
    for copy in copies:
        copy.wait()


def place_down(where, parts):
    return pl.pallas_call(
        place_kernel,
        in_specs=[SMEM] + [ANY] * 4,
        out_specs=ANY,
        out_shape=jax.ShapeDtypeStruct((1, 96, 4096), BF16),
        scratch_shapes=[pltpu.SemaphoreType.DMA((4,))],
        cost_estimate=cost(0, 2 << 20),
        compiler_params=params(),
        name="place_down",
    )(where, *parts)


def body(
    master_gate_up,
    grad_gate_up,
    first_gate_up,
    second_gate_up,
    master_down,
    grad_down,
    first_down,
    second_down,
    tokens,
    route_ids,
    route_weights,
):
    y, xh, core = lax.axis_index("y"), lax.axis_index("xh"), lax.axis_index("core")
    where = jnp.stack([y, xh, core]).astype(jnp.int32)

    near = jnp.stack([(y + 1) % 4, (y + 3) % 4, y]).astype(jnp.int32)
    dispatched = dispatch(where, near, route_ids.T, tokens)
    packed = lax.all_to_all(dispatched, ("xl", "z"), split_axis=0, concat_axis=0, tiled=True)

    gate_up = (master_gate_up, grad_gate_up, first_gate_up, second_gate_up)
    near = after(near, dispatched)
    partial, to_next, to_last, stays = adam(near, gate_up, None, 384)
    from_last, from_next, stays_across = move_y(to_next, 1), move_y(to_last, -1), move_xh(stays)
    far = ((y + 2) % 4).astype(jnp.int32)[None]
    new_master_gate_up, to_far = adam(far, gate_up, partial, 384)

    down_arrays = tuple(a[:, None] for a in (master_down, grad_down, first_down, second_down))
    whole = after(jnp.zeros((1,), jnp.int32), to_far)
    new_master_down, down = adam(whole, down_arrays, None, 1536)
    new_master_down, down = new_master_down[:, 0], down[0]

    from_last, from_next, stays_across, packed, to_far, down = staged(
        (from_last, from_next, stays_across, packed, to_far, down)
    )
    head, tail = unpack(where, packed)
    from_far, last_head, next_tail = move_y(to_far, 2), move_y(head, 1), move_y(tail, -1)
    last_across, next_across = move_xh(from_last), move_xh(from_next)
    first_four = jnp.concatenate([stays, from_last, from_next, stays_across], axis=0)
    from_far, last_head, next_tail, last_across, next_across, down, first_four, head, tail = staged(
        (from_far, last_head, next_tail, last_across, next_across, down, first_four, head, tail)
    )
    far_head, far_tail = move_y(last_head, 1), move_y(next_tail, -1)
    last_tail, next_head = move_y(tail, 1), move_y(head, -1)
    far_across = move_xh(
        jnp.concatenate([from_far, down[:768].reshape(2, 384, 256)], axis=0)
    )
    second_three = jnp.concatenate([from_far, last_across, next_across], axis=0)
    rows = [head, tail, last_head, last_tail, next_head, next_tail, far_head, far_tail]
    rows, groups, down = staged((rows, [first_four, second_three, far_across], down))
    crossed = [move_core(group) for group in groups]
    down_across = move_xh(down[768:])
    mixing = mix(after(route_ids.T, down), route_weights.T)
    hidden = last_half(where, *first_half(where, rows, groups), crossed)

    from_last, from_next = move_y(hidden, 1), move_y(hidden, -1)
    far_first, far_second = move_y(from_last[:192], 1), move_y(from_next[192:], -1)
    hiddens = [hidden, from_last, from_next, far_first, far_second]
    rest = jnp.concatenate(after([down, down_across], hidden), axis=0)
    rest_crossed = move_core(rest)
    downs = [rest, groups[2], rest_crossed, crossed[2]]
    downs, *slices = spread_down(where, downs)
    slices = [slices[0]] + [move_y(part, shift) for part, shift in zip(slices[1:], SHIFTS[1:])]
    rollout_down = place_down(where, slices)
    hiddens, rollout_down = staged((hiddens, rollout_down))
    result = second_matmul(where, hiddens, downs)
    back = lax.all_to_all(result, ("xl", "z", "y"), split_axis=0, concat_axis=0, tiled=True)
    rollout_gate_up = place_gate_up(where, groups + crossed)
    moe_out = combine(mixing, back)
    return (new_master_gate_up, new_master_down, rollout_gate_up, rollout_down, moe_out)


def solution(mesh):
    parts = jax.sharding.Mesh(mesh.devices.reshape(2, 4, 4, 2, 2), AXES)
    exp, ten = ("xl", "z"), ("y", "xh", "core")
    wide, tall, rows = P(exp, None, None, ten), P(exp, None, ten), P(AXES, None)
    return jax.shard_map(
        body,
        mesh=parts,
        in_specs=(wide,) * 4 + (tall,) * 4 + (rows,) * 3,
        out_specs=(wide, tall, P(exp, None, ten, None), P(exp, ten, None), rows),
        check_vma=False,
    )
```
